256 devices in a mesh: lat: 8 (over y, x_hi), lon: 32 (over z, x_lo, core).
Axes of the slice: x: 4 (x_hi: 2, x_lo: 2; x = x_hi * 2 + x_lo), y: 4, z: 8, core: 2. Of those that a mesh axis runs over, the one named last changes fastest.
Arguments:
- inputs: bfloat16 [64, 512, 1024], P('lat', 'lon'), may hold values from -24 to 24
- input_weight: bfloat16 [2, 1024, 1536], replicated, may hold values from -0.1875 to 0.1875
- output_weight: bfloat16 [2, 512, 1024], replicated, may hold values from -0.25 to 0.25
- norm_gain: float32 [2, 1024], replicated, may hold values from 0.1 to 1.9
- position_bias: float32 [2, 8, 49], replicated, may hold values from -6 to 260
- cotangent: bfloat16 [64, 512, 1024], P('lat', 'lon'), may hold values from -6 to 6
Outputs:
- output: bfloat16 [64, 512, 1024], P('lat', 'lon')
- input_grad: bfloat16 [64, 512, 1024], P('lat', 'lon')
- input_weight_grad: float32 [2, 1024, 1536], P(None, 'lon')
- output_weight_grad: float32 [2, 512, 1024], P(None, 'lon')
- norm_gain_grad: float32 [2, 1024], replicated
- position_bias_grad: float32 [2, 8, 49], replicated
The draws below stay inside these ranges and needn't reach their ends.
All inputs are finite; a program needn't handle non-finite values.
Results may differ from the reference program's by a relative error of at most 0.04.
Values may be sent and summed in bfloat16 or wider, within the bound.
A program may use at most 128 MiB of HBM per device.

```python
import math
import jax
import jax.numpy as jnp
from jax import lax

D = 1024
HEADS = 8
HEAD_DIM = 64
WIN = 7
LAYERS = 2
NLAT = 64
NLON = 512


def draw_inputs(key, part):
    noise_key, row_key, column_key = jax.random.split(key, 3)
    noise = jnp.clip(jax.random.normal(noise_key, (NLAT, NLON, D), jnp.float32), -4.0, 4.0)
    row_scale = jnp.exp(jax.random.uniform(row_key, (NLAT, NLON, 1), jnp.float32, math.log(0.3), math.log(3.0)))
    column_scale = jnp.exp(jax.random.uniform(column_key, (1, 1, D), jnp.float32, math.log(0.5), math.log(2.0)))
    return (noise * row_scale * column_scale).astype(jnp.bfloat16)


def draw_position_bias(key, part):
    noise_key = jax.random.fold_in(key, 0)
    bias_shape = (LAYERS, HEADS, WIN * WIN)
    return jnp.clip(jax.random.normal(noise_key, bias_shape, jnp.float32), -6.0, 6.0)


def block_levels(own_key, shape, shards, smallest, largest):
    factor_of, own = 1.0, jax.random.fold_in(own_key, 6)
    for dim, shards_of in shards:
        draws = jnp.exp(jax.random.uniform(jax.random.fold_in(own, dim), (shards_of,), jnp.float32, smallest / len(shards), largest / len(shards)))
        factor_of = factor_of * jnp.repeat(draws, shape[dim] // shards_of).reshape([-1 if axis == dim else 1 for axis in range(len(shape))])
    return factor_of


def scatter_about(key, extent, deviation, reach, cuts=(), held_as=jnp.bfloat16):
    level = block_levels(key, extent, cuts, -0.22, 0.18) if cuts else 1.0
    array = jax.random.normal(key, extent, jnp.float32) * deviation * level
    return jnp.minimum(jnp.maximum(array, -reach), reach).astype(held_as)


def setup_inputs(seed: int = 0) -> dict:
    key_of = jax.random.split(jax.random.key(seed), 7)
    inputs = draw_inputs(jax.random.fold_in(key_of[6], 71), 0)
    input_weight = scatter_about(key_of[1], (LAYERS, D, 3 * HEADS * HEAD_DIM), D ** -0.5, 0.1875)
    output_weight = scatter_about(key_of[2], (LAYERS, HEADS * HEAD_DIM, D), (HEADS * HEAD_DIM) ** -0.5, 0.25)
    norm_gain = jnp.clip(1.0 + 0.18 * jax.random.normal(key_of[3], (LAYERS, D), jnp.float32), 0.1, 1.9)
    position_bias = draw_position_bias(jax.random.fold_in(key_of[6], 71), 0)
    cotangent = scatter_about(key_of[5], (NLAT, NLON, D), 1.0, 6.0, ((0, 8), (1, 32)))
    return {"inputs": inputs, "input_weight": input_weight, "output_weight": output_weight, "norm_gain": norm_gain, "position_bias": position_bias, "cotangent": cotangent}


eps = 1e-05

def offset_list():
    radius = WIN // 2
    return [(step_lat, step_lon) for step_lat in range(-radius, radius + 1) for step_lon in range(-radius, radius + 1)]

def layer_norm(wide_input, gain):
    row_mean = lax.optimization_barrier(jnp.mean(wide_input, axis=-1, keepdims=True))
    centred = wide_input - row_mean
    variance = lax.optimization_barrier(jnp.mean(centred * centred, axis=-1, keepdims=True))
    return centred * lax.rsqrt(variance + eps) * gain

def extend(field):
    radius = WIN // 2
    wrapped = jnp.concatenate([field[:, -radius:], field, field[:, :radius]], axis=1)
    return jnp.pad(wrapped, ((radius, radius), (0, 0), (0, 0)))

def fold_back(widened):
    radius = WIN // 2
    width_all = widened.shape[1] - 2 * radius
    inner = widened[radius:-radius, radius:radius + width_all]
    inner = inner.at[:, :radius].add(widened[radius:-radius, radius + width_all:])
    inner = inner.at[:, width_all - radius:].add(widened[radius:-radius, :radius])
    return inner

def neighbour(widened, step_lat, step_lon, tile_rows, tile_cols):
    radius = WIN // 2
    return widened[radius + step_lat:radius + step_lat + tile_rows, radius + step_lon:radius + step_lon + tile_cols]

def attend(queries, keys_wide, values_wide, bias, valid_rows):
    tile_rows, tile_cols = (queries.shape[0], queries.shape[1])
    radius = WIN // 2
    score_scale = HEAD_DIM ** (-0.5)
    query_heads = queries.reshape(tile_rows, tile_cols, HEADS, HEAD_DIM).astype(jnp.float32)
    per_offset = []
    key_mask = []
    for step_lat, step_lon in offset_list():
        key_slice = neighbour(keys_wide, step_lat, step_lon, tile_rows, tile_cols)
        key_slice = key_slice.reshape(tile_rows, tile_cols, HEADS, HEAD_DIM).astype(jnp.float32)
        per_offset.append(jnp.einsum('abhd,abhd->abh', query_heads, key_slice))
        key_mask.append(valid_rows[radius + step_lat:radius + step_lat + tile_rows])
    scores = jnp.stack(per_offset, axis=-1) * score_scale + bias
    key_mask = jnp.stack(key_mask, axis=-1)[:, None, None, :]
    masked = jnp.where(key_mask, scores, -jnp.inf)
    row_max = lax.optimization_barrier(jnp.max(masked, axis=-1, keepdims=True))
    weights_exp = jnp.exp(masked - row_max)
    attention = weights_exp / lax.optimization_barrier(jnp.sum(weights_exp, axis=-1, keepdims=True))
    probs_low = attention.astype(jnp.bfloat16)
    mixed = jnp.zeros((tile_rows, tile_cols, HEADS, HEAD_DIM), jnp.float32)
    for offset_idx, (step_lat, step_lon) in enumerate(offset_list()):
        value_slice = neighbour(values_wide, step_lat, step_lon, tile_rows, tile_cols)
        value_slice = value_slice.reshape(tile_rows, tile_cols, HEADS, HEAD_DIM).astype(jnp.float32)
        mixed = mixed + probs_low[..., offset_idx, None].astype(jnp.float32) * value_slice
    return (attention, probs_low, mixed.reshape(tile_rows, tile_cols, HEADS * HEAD_DIM).astype(jnp.bfloat16))

def reference(inputs, input_weight, output_weight, norm_gain, position_bias, cotangent):
    radius = WIN // 2
    inner_width = HEADS * HEAD_DIM
    score_scale = HEAD_DIM ** (-0.5)
    lat_total, lon_total = (inputs.shape[0], inputs.shape[1])
    global_rows = jnp.arange(lat_total + 2 * radius, dtype=jnp.int32) - radius
    valid_rows = (global_rows >= 0) & (global_rows < lat_total)
    stream = inputs
    stored = []
    for layer_idx in range(LAYERS):
        wide_input = stream.astype(jnp.float32)
        normed_wide, pullback = jax.vjp(layer_norm, wide_input, norm_gain[layer_idx])
        normed = normed_wide.astype(jnp.bfloat16)
        packed = jnp.dot(normed, input_weight[layer_idx], preferred_element_type=jnp.float32).astype(jnp.bfloat16)
        queries = packed[..., :inner_width]
        keys_wide = extend(packed[..., inner_width:2 * inner_width])
        values_wide = extend(packed[..., 2 * inner_width:])
        attention, probs_low, mixed = attend(queries, keys_wide, values_wide, position_bias[layer_idx], valid_rows)
        branch = jnp.dot(mixed, output_weight[layer_idx], preferred_element_type=jnp.float32)
        stored.append((pullback, normed, queries, keys_wide, values_wide, attention, probs_low, mixed))
        stream = (wide_input + branch).astype(jnp.bfloat16)
    output = stream
    upstream = cotangent
    packed_grads = [None] * LAYERS
    output_grads = [None] * LAYERS
    gain_grads = [None] * LAYERS
    bias_grads = [None] * LAYERS
    for layer_idx in reversed(range(LAYERS)):
        pullback, normed, queries, keys_wide, values_wide, attention, probs_low, mixed = stored[layer_idx]
        output_grads[layer_idx] = jnp.einsum('abi,abd->id', mixed.astype(jnp.float32), upstream.astype(jnp.float32))
        grad_mixed = jnp.dot(upstream, output_weight[layer_idx].T, preferred_element_type=jnp.float32).astype(jnp.bfloat16)
        grad_heads = grad_mixed.reshape(lat_total, lon_total, HEADS, HEAD_DIM).astype(jnp.float32)
        query_heads = queries.reshape(lat_total, lon_total, HEADS, HEAD_DIM).astype(jnp.float32)
        per_offset = []
        for step_lat, step_lon in offset_list():
            value_slice = neighbour(values_wide, step_lat, step_lon, lat_total, lon_total)
            value_slice = value_slice.reshape(lat_total, lon_total, HEADS, HEAD_DIM).astype(jnp.float32)
            per_offset.append(jnp.einsum('abhd,abhd->abh', grad_heads, value_slice))
        grad_probs = jnp.stack(per_offset, axis=-1)
        row_delta = lax.optimization_barrier(jnp.sum(attention * grad_probs, axis=-1, keepdims=True))
        grad_scores = attention * (grad_probs - row_delta)
        bias_grads[layer_idx] = lax.optimization_barrier(jnp.sum(grad_scores, axis=(0, 1)))
        scores_low = grad_scores.astype(jnp.bfloat16)
        grad_query = jnp.zeros((lat_total, lon_total, HEADS, HEAD_DIM), jnp.float32)
        keys_acc = jnp.zeros((lat_total + 2 * radius, lon_total + 2 * radius, HEADS, HEAD_DIM), jnp.float32)
        values_acc = jnp.zeros((lat_total + 2 * radius, lon_total + 2 * radius, HEADS, HEAD_DIM), jnp.float32)
        for offset_idx, (step_lat, step_lon) in enumerate(offset_list()):
            key_slice = neighbour(keys_wide, step_lat, step_lon, lat_total, lon_total)
            key_slice = key_slice.reshape(lat_total, lon_total, HEADS, HEAD_DIM).astype(jnp.float32)
            score_piece = scores_low[..., offset_idx, None].astype(jnp.float32)
            prob_piece = probs_low[..., offset_idx, None].astype(jnp.float32)
            grad_query = grad_query + score_piece * key_slice
            row_lo = radius + step_lat
            col_lo = radius + step_lon
            keys_acc = keys_acc.at[row_lo:row_lo + lat_total, col_lo:col_lo + lon_total].add(score_piece * query_heads)
            values_acc = values_acc.at[row_lo:row_lo + lat_total, col_lo:col_lo + lon_total].add(prob_piece * grad_heads)
        grad_keys = fold_back(keys_acc) * score_scale
        grad_values = fold_back(values_acc)
        grad_packed = jnp.concatenate([(grad_query * score_scale).reshape(lat_total, lon_total, inner_width), grad_keys.reshape(lat_total, lon_total, inner_width), grad_values.reshape(lat_total, lon_total, inner_width)], axis=-1).astype(jnp.bfloat16)
        packed_grads[layer_idx] = jnp.einsum('abd,abe->de', normed.astype(jnp.float32), grad_packed.astype(jnp.float32))
        grad_normed = jnp.dot(grad_packed, input_weight[layer_idx].T, preferred_element_type=jnp.float32)
        grad_wide, gain_grad = pullback(grad_normed)
        gain_grads[layer_idx] = gain_grad
        upstream = (upstream.astype(jnp.float32) + grad_wide).astype(jnp.bfloat16)
    return (output, upstream, jnp.stack(packed_grads), jnp.stack(output_grads), jnp.stack(gain_grads), jnp.stack(bias_grads))
```

```python
import functools

import jax
import jax.numpy as jnp
import numpy as np
from jax import lax
from jax.experimental import pallas as pl
from jax.experimental.pallas import tpu as pltpu
from jax.sharding import PartitionSpec as P

HEADS = 8
HEAD_DIM = 64
WIN = 7
RADIUS = 3
LAYERS = 2
D = 1024
INNER = 512
ROWS, COLS = 8, 16
CELLS = ROWS * COLS
KEYS = 352
EPS = 1e-05
MESH = pl.DeviceIdType.MESH
F32, BF16 = jnp.float32, jnp.bfloat16

SEGMENTS = (
    (128, 48, -1, 0),
    (176, 48, 1, 0),
    (224, 32, 0, -1),
    (256, 32, 0, 1),
    (288, 16, -1, -1),
    (304, 16, -1, 1),
    (320, 16, 1, -1),
    (336, 16, 1, 1),
)


def geometry():
    key_coord = np.full((8, KEYS), 1000, np.int32)
    select = np.zeros((128, CELLS), np.float32)
    for i in range(ROWS):
        for j in range(COLS):
            key_coord[0, i * COLS + j], key_coord[1, i * COLS + j] = i, j
    for first, _, d_lat, d_lon in SEGMENTS:
        rows = {-1: range(5, 8), 0: range(8), 1: range(3)}[d_lat]
        cols = {-1: range(13, 16), 0: range(16), 1: range(3)}[d_lon]
        place = first
        for i in rows:
            for j in cols:
                key_coord[0, place], key_coord[1, place] = i + d_lat * ROWS, j + d_lon * COLS
                if d_lon != 0:
                    select[place - 224, i * COLS + j] = 1.0
                place += 1
    return key_coord, select


KEY_COORD, SELECT = geometry()


def place():
    return lax.axis_index("lat"), lax.axis_index("lon")


def at(lat, lon, d_lat, d_lon):
    return (lax.rem(lat + d_lat + 8, 8), lax.rem(lon + d_lon + 32, 32))


def greet(lat, lon):
    barrier = pltpu.get_barrier_semaphore()
    for _, _, d_lat, d_lon in SEGMENTS:
        pl.semaphore_signal(
            barrier, inc=1, device_id=at(lat, lon, d_lat, d_lon), device_id_type=MESH
        )
    return barrier


def dot(a, b, dims=((1,), (0,))):
    return lax.dot_general(a, b, (dims, ((), ())), preferred_element_type=F32)


def norm_parts(x):
    mean = jnp.mean(x, axis=-1, keepdims=True)
    centred = x - mean
    var = jnp.mean(centred * centred, axis=-1, keepdims=True)
    return centred, lax.rsqrt(var + EPS)


def split_heads(pair):
    low = lax.broadcasted_iota(jnp.int32, pair.shape, 1) < HEAD_DIM
    zero = jnp.zeros_like(pair)
    return jnp.concatenate([jnp.where(low, pair, zero), jnp.where(low, zero, pair)], axis=0)


def join_heads(both):
    low = lax.broadcasted_iota(jnp.int32, (CELLS, 2 * HEAD_DIM), 1) < HEAD_DIM
    return jnp.where(low, both[:CELLS], both[CELLS:])


def fwd_kernel(
    x_ref, win_ref, wout_ref, gain_ref, bias_ref, sel_ref, coord_ref,
    y_ref, normed_ref, q_ref, kv_ref, p_ref, mixed_ref,
    pack_ref, rw_ref, dense_ref, send_sem, recv_sem,
):
    lat, lon = place()
    barrier = greet(lat, lon)
    x = x_ref[...].astype(F32)
    centred, rstd = norm_parts(x)
    normed = (centred * rstd * gain_ref[...]).astype(BF16)
    normed_ref[...] = normed
    kv = dot(normed, win_ref[:, INNER:]).astype(BF16)
    kv_ref[0:CELLS, :] = kv
    pack_ref[...] = dot(sel_ref[...], kv).astype(BF16)
    pl.semaphore_wait(barrier, len(SEGMENTS))
    copies = []
    for n, (first, rows, d_lat, d_lon) in enumerate(SEGMENTS):
        if d_lon == 0:
            source = kv_ref.at[pl.ds(80 if d_lat < 0 else 0, rows)]
        else:
            source = pack_ref.at[pl.ds(first - 224, rows)]
        copy = pltpu.make_async_remote_copy(
            src_ref=source,
            dst_ref=kv_ref.at[pl.ds(first, rows)],
            send_sem=send_sem.at[n],
            recv_sem=recv_sem.at[n],
            device_id=at(lat, lon, -d_lat, -d_lon),
            device_id_type=MESH,
        )
        copy.start()
        copies.append(copy)
    q_ref[...] = dot(normed, win_ref[:, :INNER]).astype(BF16)
    key_i = coord_ref[0:1, :]
    row_ok = (lat * ROWS + key_i >= 0) & (lat * ROWS + key_i < 64)
    step_lat = jnp.where(row_ok, key_i, 1000) - lax.broadcasted_iota(jnp.int32, (ROWS, KEYS), 0)
    step_lon = coord_ref[1:2, :] - lax.broadcasted_iota(jnp.int32, (COLS, KEYS), 0)

    def expand(head, _):
        for w in range(WIN):
            acc = jnp.full((ROWS, KEYS), -jnp.inf, F32)
            for u in range(WIN):
                acc = jnp.where(step_lat == u - RADIUS, bias_ref[head, u * WIN + w], acc)
            rw_ref[w] = acc
        for i in range(ROWS):
            acc = jnp.full((COLS, KEYS), -jnp.inf, F32)
            for w in range(WIN):
                acc = jnp.where(step_lon == w - RADIUS, rw_ref[w, i : i + 1, :], acc)
            dense_ref[head, i * COLS : (i + 1) * COLS, :] = acc
        return 0

    lax.fori_loop(0, HEADS, expand, 0)
    for copy in copies:
        copy.wait()
    for pair in range(HEADS // 2):
        lanes = slice(pair * 128, pair * 128 + 128)
        queries = split_heads(q_ref[:, lanes])
        bias = dense_ref[2 * pair : 2 * pair + 2].reshape(2 * CELLS, KEYS)
        scores = dot(queries, kv_ref[:, lanes], ((1,), (1,))) * HEAD_DIM ** (-0.5) + bias
        top = jnp.max(scores, axis=-1, keepdims=True)
        weight = jnp.exp(scores - top)
        probs = weight / jnp.sum(weight, axis=-1, keepdims=True)
        p_ref[2 * pair : 2 * pair + 2] = probs.reshape(2, CELLS, KEYS)
        values = kv_ref[:, INNER + pair * 128 : INNER + pair * 128 + 128]
        mixed_ref[:, lanes] = join_heads(dot(probs.astype(BF16), values)).astype(BF16)
    y_ref[...] = (x + dot(mixed_ref[...], wout_ref[...])).astype(BF16)


def bwd_kernel(
    up_ref, x_ref, q_ref, kv_ref, p_ref, win_ref, wout_ref, gain_ref, sel_ref, coord_ref,
    down_ref, gp_ref, gain_grad_ref, bias_grad_ref,
    part_ref, out_ref, in_ref, ds_ref, sums_ref, send_sem, recv_sem,
):
    lat, lon = place()
    barrier = greet(lat, lon)
    up = up_ref[...]
    grad_mixed = dot(up, wout_ref[...], ((1,), (1,))).astype(BF16)
    scale = HEAD_DIM ** (-0.5)
    for pair in range(HEADS // 2):
        lanes = slice(pair * 128, pair * 128 + 128)
        vlanes = slice(INNER + pair * 128, INNER + pair * 128 + 128)
        keys = kv_ref[:, lanes]
        grads = split_heads(grad_mixed[:, lanes])
        grad_probs = dot(grads, kv_ref[:, vlanes], ((1,), (1,)))
        probs = p_ref[2 * pair : 2 * pair + 2].reshape(2 * CELLS, KEYS)
        delta = jnp.sum(probs * grad_probs, axis=-1, keepdims=True)
        grad_scores = probs * (grad_probs - delta)
        ds_ref[2 * pair : 2 * pair + 2] = grad_scores.reshape(2, CELLS, KEYS)
        scores_low = grad_scores.astype(BF16)
        gp_ref[:, lanes] = (join_heads(dot(scores_low, keys)) * scale).astype(BF16)
        grad_keys = dot(scores_low, split_heads(q_ref[:, lanes]), ((0,), (0,))) * scale
        grad_values = dot(probs.astype(BF16), grads, ((0,), (0,)))
        part_ref[:, lanes] = grad_keys[:CELLS]
        part_ref[:, vlanes] = grad_values[:CELLS]
        out_ref[:, lanes] = grad_keys[CELLS:].astype(BF16)
        out_ref[:, vlanes] = grad_values[CELLS:].astype(BF16)
    pl.semaphore_wait(barrier, len(SEGMENTS))
    copies = []
    for n, (first, rows, d_lat, d_lon) in enumerate(SEGMENTS):
        copy = pltpu.make_async_remote_copy(
            src_ref=out_ref.at[pl.ds(first - 128, rows)],
            dst_ref=in_ref.at[pl.ds(first - 128, rows)],
            send_sem=send_sem.at[n],
            recv_sem=recv_sem.at[n],
            device_id=at(lat, lon, d_lat, d_lon),
            device_id_type=MESH,
        )
        copy.start()
        copies.append(copy)
    key_i = jnp.broadcast_to(coord_ref[0:1, :], (COLS, KEYS))
    step_lon = coord_ref[1:2, :] - lax.broadcasted_iota(jnp.int32, (COLS, KEYS), 0)
    ones = jnp.ones((8, KEYS), F32)
    sums_ref[...] = jnp.zeros_like(sums_ref)

    def collect(head, _):
        for u in range(WIN):
            acc = jnp.zeros((COLS, KEYS), F32)
            for i in range(ROWS):
                acc += jnp.where(
                    key_i == i + u - RADIUS, ds_ref[head, i * COLS : (i + 1) * COLS, :], 0.0
                )
            for w in range(WIN):
                o = u * WIN + w
                sums_ref[o : o + 1, :] = jnp.sum(
                    jnp.where(step_lon == w - RADIUS, acc, 0.0), axis=0, keepdims=True
                )
        total = lax.dot_general(
            ones, sums_ref[...], (((1,), (1,)), ((), ())),
            precision=lax.Precision.HIGHEST, preferred_element_type=F32,
        )
        bias_grad_ref[head] = total
        return 0

    lax.fori_loop(0, HEADS, collect, 0)
    for copy in copies:
        copy.wait()
    part_ref[80:128, :] += in_ref[0:48, :].astype(F32)
    part_ref[0:48, :] += in_ref[48:96, :].astype(F32)
    total = part_ref[...] + dot(sel_ref[...], in_ref[96:224, :], ((0,), (0,)))
    gp_ref[:, INNER:] = total.astype(BF16)
    grad_normed = dot(gp_ref[...], win_ref[...], ((1,), (1,)))
    centred, rstd = norm_parts(x_ref[...].astype(F32))
    unit = centred * rstd
    gain_grad_ref[...] = jnp.sum(grad_normed * unit, axis=0, keepdims=True)
    scaled = grad_normed * gain_ref[...]
    mean_a = jnp.mean(scaled, axis=-1, keepdims=True)
    mean_b = jnp.mean(scaled * unit, axis=-1, keepdims=True)
    down_ref[...] = (up.astype(F32) + rstd * (scaled - mean_a - unit * mean_b)).astype(BF16)


def vmem(count):
    return [pl.BlockSpec(memory_space=pltpu.VMEM)] * count


def params(collective_id):
    return pltpu.CompilerParams(
        collective_id=collective_id, has_side_effects=True, vmem_limit_bytes=48 * 1024 * 1024
    )


def shape(dims, dtype):
    return jax.ShapeDtypeStruct(dims, dtype)


def fwd_layer(x, win, wout, gain, bias, sel, coord):
    return pl.pallas_call(
        fwd_kernel,
        out_shape=(
            shape((CELLS, D), BF16),
            shape((CELLS, D), BF16),
            shape((CELLS, INNER), BF16),
            shape((KEYS, D), BF16),
            shape((HEADS, CELLS, KEYS), F32),
            shape((CELLS, INNER), BF16),
        ),
        in_specs=vmem(4) + [pl.BlockSpec(memory_space=pltpu.SMEM)] + vmem(2),
        out_specs=tuple(vmem(6)),
        scratch_shapes=[
            pltpu.VMEM((128, D), BF16),
            pltpu.VMEM((WIN, ROWS, KEYS), F32),
            pltpu.VMEM((HEADS, CELLS, KEYS), F32),
            pltpu.SemaphoreType.DMA((8,)),
            pltpu.SemaphoreType.DMA((8,)),
        ],
        compiler_params=params(0),
    )(x, win, wout, gain, bias, sel, coord)


def bwd_layer(up, x, q, kv, p, win, wout, gain, sel, coord):
    return pl.pallas_call(
        bwd_kernel,
        out_shape=(
            shape((CELLS, D), BF16),
            shape((CELLS, 3 * INNER), BF16),
            shape((1, D), F32),
            shape((HEADS, 8, 56), F32),
        ),
        in_specs=vmem(10),
        out_specs=tuple(vmem(4)),
        scratch_shapes=[
            pltpu.VMEM((CELLS, D), F32),
            pltpu.VMEM((KEYS - CELLS, D), BF16),
            pltpu.VMEM((KEYS - CELLS, D), BF16),
            pltpu.VMEM((HEADS, CELLS, KEYS), F32),
            pltpu.VMEM((56, KEYS), F32),
            pltpu.SemaphoreType.DMA((8,)),
            pltpu.SemaphoreType.DMA((8,)),
        ],
        compiler_params=params(1),
    )(up, x, q, kv, p, win, wout, gain, sel, coord)


def shards(inputs, input_weight, output_weight, norm_gain, position_bias, cotangent):
    sel = jnp.asarray(SELECT, BF16)
    coord = jnp.asarray(KEY_COORD)
    stream = inputs.reshape(CELLS, D)
    stored = []
    for l in range(LAYERS):
        y, normed, q, kv, p, mixed = fwd_layer(
            stream, input_weight[l], output_weight[l], norm_gain[l : l + 1], position_bias[l], sel, coord
        )
        stored.append((stream, normed, q, kv, p, mixed))
        stream = y
    up = cotangent.reshape(CELLS, D)
    packed_terms, output_terms = [None] * LAYERS, [None] * LAYERS
    gain_terms, bias_terms = [None] * LAYERS, [None] * LAYERS
    for l in reversed(range(LAYERS)):
        x, normed, q, kv, p, mixed = stored[l]
        output_terms[l] = dot(mixed, up, ((0,), (0,)))
        up, gp, gain_grad, bias_grad = bwd_layer(
            up, x, q, kv, p, input_weight[l], output_weight[l], norm_gain[l : l + 1], sel, coord
        )
        packed_terms[l] = dot(normed, gp, ((0,), (0,)))
        gain_terms[l] = gain_grad[0]
        bias_terms[l] = bias_grad[:, 0, : WIN * WIN]
    lon_share = (
        lax.psum_scatter(
            jnp.stack(packed_terms).astype(jnp.bfloat16), "lon", scatter_dimension=1, tiled=True
        ),
        lax.psum_scatter(
            jnp.stack(output_terms).astype(jnp.bfloat16), "lon", scatter_dimension=1, tiled=True
        ),
    )
    packed_grad, output_grad = (
        lax.psum(lon_share[0], "lat").astype(F32),
        lax.psum(lon_share[1], "lat").astype(F32),
    )
    gain_grad, bias_grad = lax.psum((jnp.stack(gain_terms), jnp.stack(bias_terms)), ("lat", "lon"))
    tile = (ROWS, COLS, D)
    return (stream.reshape(tile), up.reshape(tile), packed_grad, output_grad, gain_grad, bias_grad)


def solution(mesh):
    return jax.shard_map(
        shards,
        mesh=mesh,
        in_specs=(P("lat", "lon", None), P(), P(), P(), P(), P("lat", "lon", None)),
        out_specs=(
            P("lat", "lon", None),
            P("lat", "lon", None),
            P(None, "lon", None),
            P(None, "lon", None),
            P(),
            P(),
        ),
        check_vma=False,
    )
```

```python
import functools

import jax
import jax.numpy as jnp
import numpy as np
from jax import lax
from jax.experimental import pallas as pl
from jax.experimental.pallas import tpu as pltpu
from jax.sharding import PartitionSpec as P

HEADS = 8
HEAD_DIM = 64
WIN = 7
RADIUS = 3
LAYERS = 2
D = 1024
INNER = 512
ROWS, COLS = 8, 16
CELLS = ROWS * COLS
KEYS = 352
EPS = 1e-05
MESH = pl.DeviceIdType.MESH
F32, BF16 = jnp.float32, jnp.bfloat16

SEGMENTS = (
    (128, 48, -1, 0),
    (176, 48, 1, 0),
    (224, 32, 0, -1),
    (256, 32, 0, 1),
    (288, 16, -1, -1),
    (304, 16, -1, 1),
    (320, 16, 1, -1),
    (336, 16, 1, 1),
)


def geometry():
    key_coord = np.full((8, KEYS), 1000, np.int32)
    select = np.zeros((128, CELLS), np.float32)
    for i in range(ROWS):
        for j in range(COLS):
            key_coord[0, i * COLS + j], key_coord[1, i * COLS + j] = i, j
    for first, _, d_lat, d_lon in SEGMENTS:
        rows = {-1: range(5, 8), 0: range(8), 1: range(3)}[d_lat]
        cols = {-1: range(13, 16), 0: range(16), 1: range(3)}[d_lon]
        place = first
        for i in rows:
            for j in cols:
                key_coord[0, place], key_coord[1, place] = i + d_lat * ROWS, j + d_lon * COLS
                if d_lon != 0:
                    select[place - 224, i * COLS + j] = 1.0
                place += 1
    return key_coord, select


KEY_COORD, SELECT = geometry()


def place():
    return lax.axis_index("lat"), lax.axis_index("lon")


def at(lat, lon, d_lat, d_lon):
    return (lax.rem(lat + d_lat + 8, 8), lax.rem(lon + d_lon + 32, 32))


def greet(lat, lon):
    barrier = pltpu.get_barrier_semaphore()
    for _, _, d_lat, d_lon in SEGMENTS:
        pl.semaphore_signal(
            barrier, inc=1, device_id=at(lat, lon, d_lat, d_lon), device_id_type=MESH
        )
    return barrier


def dot(a, b, dims=((1,), (0,))):
    return lax.dot_general(a, b, (dims, ((), ())), preferred_element_type=F32)


def norm_parts(x):
    mean = jnp.mean(x, axis=-1, keepdims=True)
    centred = x - mean
    var = jnp.mean(centred * centred, axis=-1, keepdims=True)
    return centred, lax.rsqrt(var + EPS)


def split_heads(pair):
    low = lax.broadcasted_iota(jnp.int32, pair.shape, 1) < HEAD_DIM
    zero = jnp.zeros_like(pair)
    return jnp.concatenate([jnp.where(low, pair, zero), jnp.where(low, zero, pair)], axis=0)


def join_heads(both):
    low = lax.broadcasted_iota(jnp.int32, (CELLS, 2 * HEAD_DIM), 1) < HEAD_DIM
    return jnp.where(low, both[:CELLS], both[CELLS:])


def load_weights(layer, win_hbm, wout_hbm, win_ref, wout_ref, load_sem):
    pairs = (
        (win_hbm.at[layer, :, pl.ds(INNER, 2 * INNER)], win_ref.at[:, pl.ds(INNER, 2 * INNER)]),
        (win_hbm.at[layer, :, pl.ds(0, INNER)], win_ref.at[:, pl.ds(0, INNER)]),
        (wout_hbm.at[layer], wout_ref),
    )
    loads = [pltpu.make_async_copy(src, dst, load_sem.at[n]) for n, (src, dst) in enumerate(pairs)]
    for load in loads:
        load.start()
    return loads


def fwd_kernel(
    layer, x_ref, win_hbm, wout_hbm, gain_ref, bias_ref, sel_ref, coord_ref,
    y_ref, normed_ref, q_ref, kv_ref, p_ref, mixed_ref,
    win_ref, wout_ref, pack_ref, rw_ref, dense_ref, load_sem, send_sem, recv_sem,
):
    loads = load_weights(layer, win_hbm, wout_hbm, win_ref, wout_ref, load_sem)
    lat, lon = place()
    barrier = greet(lat, lon)
    x = x_ref[...].astype(F32)
    centred, rstd = norm_parts(x)
    normed = (centred * rstd * gain_ref[...]).astype(BF16)
    normed_ref[...] = normed
    loads[0].wait()
    kv = dot(normed, win_ref[:, INNER:]).astype(BF16)
    kv_ref[0:CELLS, :] = kv
    pack_ref[...] = dot(sel_ref[...], kv).astype(BF16)
    pl.semaphore_wait(barrier, len(SEGMENTS))
    copies = []
    for n, (first, rows, d_lat, d_lon) in enumerate(SEGMENTS):
        if d_lon == 0:
            source = kv_ref.at[pl.ds(80 if d_lat < 0 else 0, rows)]
        else:
            source = pack_ref.at[pl.ds(first - 224, rows)]
        copy = pltpu.make_async_remote_copy(
            src_ref=source,
            dst_ref=kv_ref.at[pl.ds(first, rows)],
            send_sem=send_sem.at[n],
            recv_sem=recv_sem.at[n],
            device_id=at(lat, lon, -d_lat, -d_lon),
            device_id_type=MESH,
        )
        copy.start()
        copies.append(copy)
    loads[1].wait()
    q_ref[...] = dot(normed, win_ref[:, :INNER]).astype(BF16)
    key_i = coord_ref[0:1, :]
    row_ok = (lat * ROWS + key_i >= 0) & (lat * ROWS + key_i < 64)
    step_lat = jnp.where(row_ok, key_i, 1000) - lax.broadcasted_iota(jnp.int32, (ROWS, KEYS), 0)
    step_lon = coord_ref[1:2, :] - lax.broadcasted_iota(jnp.int32, (COLS, KEYS), 0)

    def expand(head, _):
        for w in range(WIN):
            acc = jnp.full((ROWS, KEYS), -jnp.inf, F32)
            for u in range(WIN):
                acc = jnp.where(step_lat == u - RADIUS, bias_ref[head, u * WIN + w], acc)
            rw_ref[w] = acc
        for i in range(ROWS):
            acc = jnp.full((COLS, KEYS), -jnp.inf, F32)
            for w in range(WIN):
                acc = jnp.where(step_lon == w - RADIUS, rw_ref[w, i : i + 1, :], acc)
            dense_ref[head, i * COLS : (i + 1) * COLS, :] = acc
        return 0

    lax.fori_loop(0, HEADS, expand, 0)
    for copy in copies:
        copy.wait()
    for pair in range(HEADS // 2):
        lanes = slice(pair * 128, pair * 128 + 128)
        queries = split_heads(q_ref[:, lanes])
        bias = dense_ref[2 * pair : 2 * pair + 2].reshape(2 * CELLS, KEYS)
        scores = dot(queries, kv_ref[:, lanes], ((1,), (1,))) * HEAD_DIM ** (-0.5) + bias
        top = jnp.max(scores, axis=-1, keepdims=True)
        weight = jnp.exp(scores - top)
        probs = weight / jnp.sum(weight, axis=-1, keepdims=True)
        p_ref[2 * pair : 2 * pair + 2] = probs.reshape(2, CELLS, KEYS)
        values = kv_ref[:, INNER + pair * 128 : INNER + pair * 128 + 128]
        mixed_ref[:, lanes] = join_heads(dot(probs.astype(BF16), values)).astype(BF16)
    loads[2].wait()
    y_ref[...] = (x + dot(mixed_ref[...], wout_ref[...])).astype(BF16)


def bwd_kernel(
    layer, up_ref, x_ref, q_ref, kv_ref, p_ref, win_hbm, wout_hbm, gain_ref, sel_ref, coord_ref,
    down_ref, gp_ref, gain_grad_ref, bias_grad_ref,
    win_ref, wout_ref, part_ref, out_ref, in_ref, ds_ref, sums_ref, load_sem, send_sem, recv_sem,
):
    loads = load_weights(layer, win_hbm, wout_hbm, win_ref, wout_ref, load_sem)
    lat, lon = place()
    barrier = greet(lat, lon)
    up = up_ref[...]
    loads[2].wait()
    grad_mixed = dot(up, wout_ref[...], ((1,), (1,))).astype(BF16)
    scale = HEAD_DIM ** (-0.5)
    for pair in range(HEADS // 2):
        lanes = slice(pair * 128, pair * 128 + 128)
        vlanes = slice(INNER + pair * 128, INNER + pair * 128 + 128)
        keys = kv_ref[:, lanes]
        grads = split_heads(grad_mixed[:, lanes])
        grad_probs = dot(grads, kv_ref[:, vlanes], ((1,), (1,)))
        probs = p_ref[2 * pair : 2 * pair + 2].reshape(2 * CELLS, KEYS)
        delta = jnp.sum(probs * grad_probs, axis=-1, keepdims=True)
        grad_scores = probs * (grad_probs - delta)
        ds_ref[2 * pair : 2 * pair + 2] = grad_scores.reshape(2, CELLS, KEYS)
        scores_low = grad_scores.astype(BF16)
        gp_ref[:, lanes] = (join_heads(dot(scores_low, keys)) * scale).astype(BF16)
        grad_keys = dot(scores_low, split_heads(q_ref[:, lanes]), ((0,), (0,))) * scale
        grad_values = dot(probs.astype(BF16), grads, ((0,), (0,)))
        part_ref[:, lanes] = grad_keys[:CELLS]
        part_ref[:, vlanes] = grad_values[:CELLS]
        out_ref[:, lanes] = grad_keys[CELLS:].astype(BF16)
        out_ref[:, vlanes] = grad_values[CELLS:].astype(BF16)
    pl.semaphore_wait(barrier, len(SEGMENTS))
    copies = []
    for n, (first, rows, d_lat, d_lon) in enumerate(SEGMENTS):
        copy = pltpu.make_async_remote_copy(
            src_ref=out_ref.at[pl.ds(first - 128, rows)],
            dst_ref=in_ref.at[pl.ds(first - 128, rows)],
            send_sem=send_sem.at[n],
            recv_sem=recv_sem.at[n],
            device_id=at(lat, lon, d_lat, d_lon),
            device_id_type=MESH,
        )
        copy.start()
        copies.append(copy)
    key_i = jnp.broadcast_to(coord_ref[0:1, :], (COLS, KEYS))
    step_lon = coord_ref[1:2, :] - lax.broadcasted_iota(jnp.int32, (COLS, KEYS), 0)
    ones = jnp.ones((8, KEYS), F32)
    sums_ref[...] = jnp.zeros_like(sums_ref)

    def collect(head, _):
        for u in range(WIN):
            acc = jnp.zeros((COLS, KEYS), F32)
            for i in range(ROWS):
                acc += jnp.where(
                    key_i == i + u - RADIUS, ds_ref[head, i * COLS : (i + 1) * COLS, :], 0.0
                )
            for w in range(WIN):
                o = u * WIN + w
                sums_ref[o : o + 1, :] = jnp.sum(
                    jnp.where(step_lon == w - RADIUS, acc, 0.0), axis=0, keepdims=True
                )
        total = lax.dot_general(
            ones, sums_ref[...], (((1,), (1,)), ((), ())),
            precision=lax.Precision.HIGHEST, preferred_element_type=F32,
        )
        bias_grad_ref[pl.ds(head, 1), :] = total[0:1]
        return 0

    lax.fori_loop(0, HEADS, collect, 0)
    for copy in copies:
        copy.wait()
    part_ref[80:128, :] += in_ref[0:48, :].astype(F32)
    part_ref[0:48, :] += in_ref[48:96, :].astype(F32)
    total = part_ref[...] + dot(sel_ref[...], in_ref[96:224, :], ((0,), (0,)))
    gp_ref[:, INNER:] = total.astype(BF16)
    loads[0].wait()
    loads[1].wait()
    grad_normed = dot(gp_ref[...], win_ref[...], ((1,), (1,)))
    centred, rstd = norm_parts(x_ref[...].astype(F32))
    unit = centred * rstd
    gain_grad_ref[...] = jnp.sum(grad_normed * unit, axis=0, keepdims=True)
    scaled = grad_normed * gain_ref[...]
    mean_a = jnp.mean(scaled, axis=-1, keepdims=True)
    mean_b = jnp.mean(scaled * unit, axis=-1, keepdims=True)
    down_ref[...] = (up.astype(F32) + rstd * (scaled - mean_a - unit * mean_b)).astype(BF16)


def vmem(count):
    return [pl.BlockSpec(memory_space=pltpu.VMEM)] * count


def anywhere(count):
    return [pl.BlockSpec(memory_space=pl.ANY)] * count


def params(collective_id):
    return pltpu.CompilerParams(
        collective_id=collective_id, has_side_effects=True, vmem_limit_bytes=48 * 1024 * 1024
    )


def shape(dims, dtype):
    return jax.ShapeDtypeStruct(dims, dtype)


def fwd_layer(layer, x, win, wout, gain, bias, sel, coord):
    return pl.pallas_call(
        functools.partial(fwd_kernel, layer),
        out_shape=(
            shape((CELLS, D), BF16),
            shape((CELLS, D), BF16),
            shape((CELLS, INNER), BF16),
            shape((KEYS, D), BF16),
            shape((HEADS, CELLS, KEYS), F32),
            shape((CELLS, INNER), BF16),
        ),
        in_specs=vmem(1) + anywhere(2) + vmem(1) + [pl.BlockSpec(memory_space=pltpu.SMEM)] + vmem(2),
        out_specs=tuple(vmem(6)),
        scratch_shapes=[
            pltpu.VMEM((D, 3 * INNER), BF16),
            pltpu.VMEM((INNER, D), BF16),
            pltpu.VMEM((128, D), BF16),
            pltpu.VMEM((WIN, ROWS, KEYS), F32),
            pltpu.VMEM((HEADS, CELLS, KEYS), F32),
            pltpu.SemaphoreType.DMA((3,)),
            pltpu.SemaphoreType.DMA((8,)),
            pltpu.SemaphoreType.DMA((8,)),
        ],
        compiler_params=params(layer),
    )(x, win, wout, gain, bias, sel, coord)


def bwd_layer(layer, up, x, q, kv, p, win, wout, gain, sel, coord):
    return pl.pallas_call(
        functools.partial(bwd_kernel, layer),
        out_shape=(
            shape((CELLS, D), BF16),
            shape((CELLS, 3 * INNER), BF16),
            shape((1, D), F32),
            shape((HEADS, 56), F32),
        ),
        in_specs=vmem(5) + anywhere(2) + vmem(3),
        out_specs=tuple(vmem(4)),
        scratch_shapes=[
            pltpu.VMEM((D, 3 * INNER), BF16),
            pltpu.VMEM((INNER, D), BF16),
            pltpu.VMEM((CELLS, D), F32),
            pltpu.VMEM((KEYS - CELLS, D), BF16),
            pltpu.VMEM((KEYS - CELLS, D), BF16),
            pltpu.VMEM((HEADS, CELLS, KEYS), F32),
            pltpu.VMEM((56, KEYS), F32),
            pltpu.SemaphoreType.DMA((3,)),
            pltpu.SemaphoreType.DMA((8,)),
            pltpu.SemaphoreType.DMA((8,)),
        ],
        compiler_params=params(3 - layer),
    )(up, x, q, kv, p, win, wout, gain, sel, coord)


def hop(index, step):
    if step == 1:
        return index + 1 - 2 * lax.rem(index, 2)
    if step == 2:
        return lax.rem(index + 2, 4)
    return 3 - index


def chip():
    lat, lon = place()
    x = 2 * lax.rem(lat, 2) + lax.rem(lax.div(lon, 2), 2)
    return x, lax.div(lat, 2), lax.div(lon, 4), lax.rem(lon, 2)


def device(x, y, z, core):
    return (2 * y + lax.div(x, 2), 4 * z + 2 * lax.rem(x, 2) + core)


ORDER = ((1, 3), (3, 1), (1, 3), (3, 1))


def slot_of(core, index, x_low):
    part = 2 * core + index // 8
    x, y = 2 * ((index % 8) // 4) + x_low, index % 4
    return (part, x, y) if part < 2 else (part, y, x)


def add(a, b):
    return (a.astype(F32) + b.astype(F32)).astype(BF16)


class Sum:
    def __init__(self, layer, refs, bufs, send_sem, recv_sem):
        self.l, self.refs, self.b = layer, refs, bufs
        self.send_sem, self.recv_sem, self.count, self.copies = send_sem, recv_sem, 0, []

    def send(self, src, dst, to):
        copy = pltpu.make_async_remote_copy(
            src_ref=src,
            dst_ref=dst,
            send_sem=self.send_sem.at[self.l, self.count],
            recv_sem=self.recv_sem.at[self.l, self.count],
            device_id=to,
            device_id_type=MESH,
        )
        copy.start()
        self.count += 1
        self.copies.append(copy)

    def wait(self):
        for copy in self.copies:
            copy.wait()
        self.copies = []

    def share(self):
        x, y, z, core = chip()
        l, b = self.l, self.b
        normed, packed, mixed, up = self.refs
        to = device(x, y, z, 1 - core)
        self.send(normed, b["nb"].at[l, pl.ds(CELLS, CELLS)], to)
        self.send(mixed, b["mb"].at[l, pl.ds(CELLS, CELLS)], to)
        other, mine = 1 - core, core
        half = lambda ref, which, width: ref.at[:, pl.ds(pl.multiple_of(which * width, 128), width)]
        self.send(half(up, other, 512), b["ub"].at[l, pl.ds(CELLS, CELLS)], to)
        self.send(half(packed, other, 768), b["gb"].at[l, pl.ds(CELLS, CELLS)], to)
        b["nb"][l, :CELLS] = normed[...]
        b["mb"][l, :CELLS] = mixed[...]
        b["ub"][l, :CELLS] = half(up, mine, 512)[...]
        b["gb"][l, :CELLS] = half(packed, mine, 768)[...]

    def product(self):
        self.wait()
        l, b = self.l, self.b
        slab = b["slab"]

        def step(k, _):
            for zz in range(2):
                z = 2 * k + zz
                left = b["nb"][l, :, pl.ds(pl.multiple_of(z * 128, 128), 128)]
                term = dot(left, b["gb"][l], ((0,), (0,))).astype(BF16)
                for x_low in range(2):
                    for rg in range(4):
                        for cg in range(6):
                            part, f, g = slot_of(rg // 2, (rg % 2) * 6 + cg, x_low)
                            row = x_low * 64 + rg * 16
                            slab[l, part, f, g, z] = term[row : row + 16, cg * 128 : cg * 128 + 128]
            left = b["mb"][l, :, pl.ds(pl.multiple_of(k * 128, 128), 128)]
            term = dot(left, b["ub"][l], ((0,), (0,))).astype(BF16)
            for zz in range(2):
                for x_low in range(2):
                    for core in range(2):
                        for cg in range(4):
                            part, f, g = slot_of(core, 12 + cg, x_low)
                            row = zz * 64 + x_low * 32 + core * 16
                            slab[l, part, f, g, 2 * k + zz] = term[
                                row : row + 16, cg * 128 : cg * 128 + 128
                            ]
            return 0

        lax.fori_loop(0, 4, step, 0)
        x, y, z, core = chip()
        for t in range(4):
            f = x if t < 2 else y
            for k, step_of in enumerate((ORDER[t][0], 2)):
                self.send(slab.at[l, t, hop(f, step_of)], b["r1"].at[l, t, k], self.peer(t, 0))

    def peer(self, t, turn, second=False):
        x, y, z, core = chip()
        step = ORDER[t][turn]
        if (t < 2) != second:
            return device(hop(x, step), y, z, core)
        return device(x, hop(y, step), z, core)

    def stage(self, number):
        self.wait()
        l, b = self.l, self.b
        slab = b["slab"]
        x, y, z, core = chip()
        if number <= 4:
            for t in range(4):
                f, g = (x, y) if t < 2 else (y, x)
                last = ORDER[t][1]
                if number == 1:
                    slab[l, t, f] = add(slab[l, t, f], b["r1"][l, t, 0])
                    nxt = hop(f, last)
                    slab[l, t, nxt] = add(slab[l, t, nxt], b["r1"][l, t, 1])
                    self.send(slab.at[l, t, nxt], b["r2"].at[l, t], self.peer(t, 1))
                elif number == 2:
                    slab[l, t, f] = add(slab[l, t, f], b["r2"][l, t])
                    for k, step_of in enumerate((ORDER[t][0], 2)):
                        self.send(
                            slab.at[l, t, f, hop(g, step_of)], b["r3"].at[l, t, k], self.peer(t, 0, True)
                        )
                elif number == 3:
                    slab[l, t, f, g] = add(slab[l, t, f, g], b["r3"][l, t, 0])
                    nxt = hop(g, last)
                    slab[l, t, f, nxt] = add(slab[l, t, f, nxt], b["r3"][l, t, 1])
                    self.send(slab.at[l, t, f, nxt], b["r4"].at[l, t], self.peer(t, 1, True))
                else:
                    b["zs"][l, :, t] = add(slab[l, t, f, g], b["r4"][l, t])
            if number == 4:
                b["zr"][l, z] = b["zs"][l, z]
                for d in range(1, 8):
                    to = lax.rem(z + d, 8)
                    self.send(b["zs"].at[l, to], b["zr"].at[l, z], device(x, y, to, core))
        elif number == 5:
            total = b["zr"][l, 0].astype(F32)
            for k in range(1, 8):
                total += b["zr"][l, k].astype(F32)
            b["fin"][l] = total.astype(BF16)
            x_high, x_low = lax.div(x, 2), lax.rem(x, 2)
            own = 8 * core + 4 * x_high + y
            b["ag"][l, own] = b["fin"][l, pl.ds(2 * core, 2)]
            for d in range(1, 16):
                to_core = 1 - core if d // 8 else core
                to_high = 1 - x_high if (d // 4) % 2 else x_high
                to_y = lax.rem(y + d % 4, 4)
                self.send(
                    b["fin"].at[l, pl.ds(2 * to_core, 2)],
                    b["ag"].at[l, own],
                    device(2 * to_high + x_low, to_y, z, to_core),
                )
        else:
            in_out, out_out = b["in_out"], b["out_out"]
            for slot in range(16):
                core_of, rest = slot // 8, slot % 8
                for half in range(2):
                    index = half * 8 + rest
                    tile = b["ag"][l, slot, half].astype(F32)
                    if index < 12:
                        row, col = 16 * (index // 6), core_of * 768 + (index % 6) * 128
                        in_out[l, row : row + 16, col : col + 128] = tile
                    else:
                        col = core_of * 512 + (index - 12) * 128
                        out_out[l, :, col : col + 128] = tile


def sum_kernel(*args):
    refs = [args[0:4], args[4:8]]
    small = [args[8:10], args[10:12]]
    in_out, out_out, gain_out, bias_out = args[12:16]
    names = ("nb", "mb", "ub", "gb", "slab", "r1", "r2", "r3", "r4", "zs", "zr", "fin", "ag")
    bufs = dict(zip(names, args[16:29]))
    bufs["in_out"], bufs["out_out"] = in_out, out_out
    vec, vec_in, vec_z, send_sem, recv_sem, vec_send, vec_recv = args[29:]
    x, y, z, core = chip()
    x_high, x_low = lax.div(x, 2), lax.rem(x, 2)
    barrier = pltpu.get_barrier_semaphore()
    peers = []
    for d in range(1, 16):
        to_core = 1 - core if d // 8 else core
        to_high = 1 - x_high if (d // 4) % 2 else x_high
        peers.append(device(2 * to_high + x_low, lax.rem(y + d % 4, 4), z, to_core))
    for d in (1, 3):
        peers.append(device(hop(x, d), y, z, core))
    for d in range(1, 8):
        peers.append(device(x, y, lax.rem(z + d, 8), core))
    for to in peers:
        pl.semaphore_signal(barrier, inc=1, device_id=to, device_id_type=MESH)
    vec[...] = jnp.zeros_like(vec)
    for l in range(LAYERS):
        gain_grad, bias_grad = small[l]
        for k in range(8):
            vec[8 * l + k : 8 * l + k + 1, :] = gain_grad[:, k * 128 : k * 128 + 128]
        vec[16 + 8 * l : 24 + 8 * l, 0:56] = bias_grad[...]
    pl.semaphore_wait(barrier, len(peers))

    def vec_send_to(n, dst, to):
        copy = pltpu.make_async_remote_copy(
            src_ref=vec, dst_ref=dst, send_sem=vec_send.at[n], recv_sem=vec_recv.at[n],
            device_id=to, device_id_type=MESH,
        )
        copy.start()
        return copy

    vec_peers = (
        device(x, y, z, 1 - core),
        device(hop(x, 1), y, z, core),
        device(hop(x, 3), y, z, core),
        device(x, hop(y, 1), z, core),
        device(x, hop(y, 3), z, core),
    )
    sums = [Sum(l, refs[l], bufs, send_sem, recv_sem) for l in range(LAYERS)]
    sums[1].share()
    sums[0].share()
    copy = vec_send_to(0, vec_in.at[0], vec_peers[0])
    sums[1].product()
    sums[0].product()
    for number in range(1, 7):
        sums[1].stage(number)
        sums[0].stage(number)
        if number <= 5:
            copy.wait()
            vec[...] += vec_in[number - 1]
            if number < 5:
                copy = vec_send_to(number, vec_in.at[number], vec_peers[number])
            else:
                vec_z[z] = vec[...]
                copies = [
                    vec_send_to(4 + d, vec_z.at[z], device(x, y, lax.rem(z + d, 8), core))
                    for d in range(1, 8)
                ]
    for copy in copies:
        copy.wait()
    total = vec_z[0]
    for k in range(1, 8):
        total += vec_z[k]
    for l in range(LAYERS):
        for k in range(8):
            gain_out[l : l + 1, k * 128 : k * 128 + 128] = total[8 * l + k : 8 * l + k + 1]
        bias_out[l] = total[16 + 8 * l : 24 + 8 * l, : WIN * WIN]


def sum_all(layers, small):
    tile = (16, 128)
    return pl.pallas_call(
        sum_kernel,
        out_shape=(
            shape((LAYERS, 32, 1536), F32),
            shape((LAYERS, 16, 1024), F32),
            shape((LAYERS, D), F32),
            shape((LAYERS, HEADS, WIN * WIN), F32),
        ),
        in_specs=vmem(12),
        out_specs=tuple(vmem(4)),
        scratch_shapes=[
            pltpu.VMEM((2, 2 * CELLS, D), BF16),
            pltpu.VMEM((2, 2 * CELLS, INNER), BF16),
            pltpu.VMEM((2, 2 * CELLS, 512), BF16),
            pltpu.VMEM((2, 2 * CELLS, 768), BF16),
            pltpu.VMEM((2, 4, 4, 4, 8) + tile, BF16),
            pltpu.VMEM((2, 4, 2, 4, 8) + tile, BF16),
            pltpu.VMEM((2, 4, 4, 8) + tile, BF16),
            pltpu.VMEM((2, 4, 2, 8) + tile, BF16),
            pltpu.VMEM((2, 4, 8) + tile, BF16),
            pltpu.VMEM((2, 8, 4) + tile, BF16),
            pltpu.VMEM((2, 8, 4) + tile, BF16),
            pltpu.VMEM((2, 4) + tile, BF16),
            pltpu.VMEM((2, 16, 2) + tile, BF16),
            pltpu.VMEM((32, 128), F32),
            pltpu.VMEM((5, 32, 128), F32),
            pltpu.VMEM((8, 32, 128), F32),
            pltpu.SemaphoreType.DMA((2, 50)),
            pltpu.SemaphoreType.DMA((2, 50)),
            pltpu.SemaphoreType.DMA((12,)),
            pltpu.SemaphoreType.DMA((12,)),
        ],
        compiler_params=params(4),
    )(*layers[0], *layers[1], *small[0], *small[1])


def shards(inputs, input_weight, output_weight, norm_gain, position_bias, cotangent):
    sel = jnp.asarray(SELECT, BF16)
    coord = jnp.asarray(KEY_COORD)
    stream = inputs.reshape(CELLS, D)
    stored = []
    for l in range(LAYERS):
        y, normed, q, kv, p, mixed = fwd_layer(
            l, stream, input_weight, output_weight, norm_gain[l : l + 1], position_bias[l], sel, coord
        )
        stored.append((stream, normed, q, kv, p, mixed))
        stream = y
    up = cotangent.reshape(CELLS, D)
    terms, small = [None] * LAYERS, [None] * LAYERS
    for l in reversed(range(LAYERS)):
        x, normed, q, kv, p, mixed = stored[l]
        down, packed, gain_grad, bias_grad = bwd_layer(
            l, up, x, q, kv, p, input_weight, output_weight, norm_gain[l : l + 1], sel, coord
        )
        terms[l] = (normed, packed, mixed, up)
        small[l] = (gain_grad, bias_grad)
        up = down
    packed_grad, output_grad, gain_grad, bias_grad = sum_all(terms, small)
    tile = (ROWS, COLS, D)
    return (stream.reshape(tile), up.reshape(tile), packed_grad, output_grad, gain_grad, bias_grad)


def solution(mesh):
    return jax.shard_map(
        shards,
        mesh=mesh,
        in_specs=(P("lat", "lon", None), P(), P(), P(), P(), P("lat", "lon", None)),
        out_specs=(
            P("lat", "lon", None),
            P("lat", "lon", None),
            P(None, "lon", None),
            P(None, "lon", None),
            P(),
            P(),
        ),
        check_vma=False,
    )
```

```python
import jax
import jax.numpy as jnp
import numpy as np
from jax import lax
from jax.experimental import pallas as pl
from jax.experimental.pallas import tpu as pltpu
from jax.sharding import PartitionSpec as P

HEADS = 8
HEAD_DIM = 64
WIN = 7
RADIUS = 3
LAYERS = 2
D = 1024
INNER = 512
ROWS, COLS = 8, 16
CELLS = ROWS * COLS
KEYS = 352
EPS = 1e-05
MESH = pl.DeviceIdType.MESH
F32, BF16 = jnp.float32, jnp.bfloat16

SEGMENTS = (
    (128, 48, -1, 0),
    (176, 48, 1, 0),
    (224, 32, 0, -1),
    (256, 32, 0, 1),
    (288, 16, -1, -1),
    (304, 16, -1, 1),
    (320, 16, 1, -1),
    (336, 16, 1, 1),
)


def geometry():
    key_coord = np.full((8, KEYS), 1000, np.int32)
    select = np.zeros((128, CELLS), np.float32)
    for i in range(ROWS):
        for j in range(COLS):
            key_coord[0, i * COLS + j], key_coord[1, i * COLS + j] = i, j
    for first, _, d_lat, d_lon in SEGMENTS:
        rows = {-1: range(5, 8), 0: range(8), 1: range(3)}[d_lat]
        cols = {-1: range(13, 16), 0: range(16), 1: range(3)}[d_lon]
        place = first
        for i in rows:
            for j in cols:
                key_coord[0, place], key_coord[1, place] = i + d_lat * ROWS, j + d_lon * COLS
                if d_lon != 0:
                    select[place - 224, i * COLS + j] = 1.0
                place += 1
    return key_coord, select


KEY_COORD, SELECT = geometry()


def place():
    return lax.axis_index("lat"), lax.axis_index("lon")


def at(lat, lon, d_lat, d_lon):
    return (lax.rem(lat + d_lat + 8, 8), lax.rem(lon + d_lon + 32, 32))


def dot(a, b, dims=((1,), (0,))):
    return lax.dot_general(a, b, (dims, ((), ())), preferred_element_type=F32)


def norm_parts(x):
    mean = jnp.mean(x, axis=-1, keepdims=True)
    centred = x - mean
    var = jnp.mean(centred * centred, axis=-1, keepdims=True)
    return centred, lax.rsqrt(var + EPS)


def split_heads(pair):
    low = lax.broadcasted_iota(jnp.int32, pair.shape, 1) < HEAD_DIM
    zero = jnp.zeros_like(pair)
    return jnp.concatenate([jnp.where(low, pair, zero), jnp.where(low, zero, pair)], axis=0)


def join_heads(both):
    low = lax.broadcasted_iota(jnp.int32, (CELLS, 2 * HEAD_DIM), 1) < HEAD_DIM
    return jnp.where(low, both[:CELLS], both[CELLS:])


def chip():
    lat, lon = place()
    x = 2 * lax.rem(lat, 2) + lax.rem(lax.div(lon, 2), 2)
    return x, lax.div(lat, 2), lax.div(lon, 4), lax.rem(lon, 2)


def device(x, y, z, core):
    return (2 * y + lax.div(x, 2), 4 * z + 2 * lax.rem(x, 2) + core)


def turn(index, step, count):
    return lax.rem(index + step, count)


def owners():
    x, y, z, core = chip()
    x_high, x_low = lax.div(x, 2), lax.rem(x, 2)
    for d in range(1, 16):
        to_core = 1 - core if d // 8 else core
        to_high = 1 - x_high if (d // 4) % 2 else x_high
        yield device(2 * to_high + x_low, turn(y, d % 4, 4), z, to_core), to_core


def across():
    x, y, z, core = chip()
    x_high, x_low = lax.div(x, 2), lax.rem(x, 2)
    for d in range(1, 16):
        to_low = 1 - x_low if d % 2 else x_low
        yield device(2 * x_high + to_low, y, turn(z, d // 2, 8), core)


def greet():
    lat, lon = place()
    x, y, z, core = chip()
    peers = [to for to, _ in owners()] + list(across()) + [device(3 - x, y, z, core)]
    peers += [at(lat, lon, d_lat, d_lon) for _, _, d_lat, d_lon in SEGMENTS if d_lon != 0]
    barrier = pltpu.get_barrier_semaphore()
    for to in peers:
        pl.semaphore_signal(barrier, inc=1, device_id=to, device_id_type=MESH)
    return barrier, len(peers)


X_FIRST = (True, False, False, True)
EARLY, LATE = (0, 2), (1, 3)


def slot_of(core, late, index, x_low):
    part = 2 * core + late
    x, y = 2 * (index // 4) + x_low, index % 4
    return (part, x, y) if X_FIRST[part] else (part, y, x)


class Sender:
    def __init__(self, send_sem, recv_sem):
        self.send_sem, self.recv_sem, self.count = send_sem, recv_sem, 0

    def __call__(self, src, dst, to):
        copy = pltpu.make_async_remote_copy(
            src_ref=src,
            dst_ref=dst,
            send_sem=self.send_sem.at[self.count],
            recv_sem=self.recv_sem.at[self.count],
            device_id=to,
            device_id_type=MESH,
        )
        copy.start()
        self.count += 1
        return copy


class Layer:
    def __init__(self, l, b, send, loads):
        self.l, self.b, self.send, self.loads = l, b, send, loads
        self.copies, self.vec_copies, self.pending = [], [], [0, 1, 2]
        self.shares, self.moves = [], {EARLY: [], LATE: [], "z": []}

    def load(self, n):
        if n in self.pending:
            self.pending.remove(n)
            self.loads[n].wait()

    def forward_start(self, x, before_send):
        b, l = self.b, self.l
        lat, lon = place()
        centred, rstd = norm_parts(x)
        normed = (centred * rstd * b["gain"][l : l + 1, :]).astype(BF16)
        b["normed"][l] = normed
        self.load(0)
        kv = dot(normed, b["win"][l, :, INNER:]).astype(BF16)
        b["kv"][l, 0:CELLS, :] = kv
        b["pack"][l] = dot(b["sel"][...], kv).astype(BF16)
        before_send()
        for first, rows, d_lat, d_lon in SEGMENTS:
            if d_lon == 0:
                source = b["kv"].at[l, pl.ds(80 if d_lat < 0 else 0, rows)]
            else:
                source = b["pack"].at[l, pl.ds(first - 224, rows)]
            to = at(lat, lon, -d_lat, -d_lon)
            self.copies.append(self.send(source, b["kv"].at[l, pl.ds(first, rows)], to))
        self.load(1)
        b["q"][l] = dot(normed, b["win"][l, :, :INNER]).astype(BF16)
        self.expand()

    def expand(self):
        b, l = self.b, self.l
        lat, lon = place()
        key_i = b["coord"][0:1, :]
        row_ok = (lat * ROWS + key_i >= 0) & (lat * ROWS + key_i < 64)
        step_lat = jnp.where(row_ok, key_i, 1000) - lax.broadcasted_iota(jnp.int32, (ROWS, KEYS), 0)
        step_lon = b["coord"][1:2, :] - lax.broadcasted_iota(jnp.int32, (COLS, KEYS), 0)
        bias, rw, dense = b["bias"], b["rw"], b["dense"]

        def step(head, _):
            for w in range(WIN):
                acc = jnp.full((ROWS, KEYS), -jnp.inf, F32)
                for u in range(WIN):
                    acc = jnp.where(step_lat == u - RADIUS, bias[l, head, u * WIN + w], acc)
                rw[w] = acc
            for i in range(ROWS):
                acc = jnp.full((COLS, KEYS), -jnp.inf, F32)
                for w in range(WIN):
                    acc = jnp.where(step_lon == w - RADIUS, rw[w, i : i + 1, :], acc)
                dense[head, i * COLS : (i + 1) * COLS, :] = acc
            return 0

        lax.fori_loop(0, HEADS, step, 0)

    def wait(self):
        for copy in self.copies:
            copy.wait()
        self.copies = []

    def forward_end(self, x):
        b, l = self.b, self.l
        self.wait()
        kv = b["kv"]
        for pair in range(HEADS // 2):
            lanes = slice(pair * 128, pair * 128 + 128)
            queries = split_heads(b["q"][l, :, lanes])
            bias = b["dense"][2 * pair : 2 * pair + 2].reshape(2 * CELLS, KEYS)
            scores = dot(queries, kv[l, :, lanes], ((1,), (1,))) * HEAD_DIM ** (-0.5) + bias
            top = jnp.max(scores, axis=-1, keepdims=True)
            weight = jnp.exp(scores - top)
            probs = weight / jnp.sum(weight, axis=-1, keepdims=True)
            b["probs"][l, 2 * pair : 2 * pair + 2] = probs.reshape(2, CELLS, KEYS)
            values = kv[l, :, INNER + pair * 128 : INNER + pair * 128 + 128]
            b["mixed"][l, :, lanes] = join_heads(dot(probs.astype(BF16), values)).astype(BF16)
        self.load(2)
        return (x + dot(b["mixed"][l], b["wout"][l])).astype(BF16)

    def mixed_grad(self, up):
        self.b["gm"][self.l] = dot(up, self.b["wout"][self.l], ((1,), (1,))).astype(BF16)

    def backward_start(self):
        b, l = self.b, self.l
        lat, lon = place()
        scale = HEAD_DIM ** (-0.5)
        kv, packed, part, out = b["kv"], b["packed"], b["part"], b["out"]
        for pair in range(HEADS // 2):
            lanes = slice(pair * 128, pair * 128 + 128)
            vlanes = slice(INNER + pair * 128, INNER + pair * 128 + 128)
            keys = kv[l, :, lanes]
            grads = split_heads(b["gm"][l, :, lanes])
            grad_probs = dot(grads, kv[l, :, vlanes], ((1,), (1,)))
            probs = b["probs"][l, 2 * pair : 2 * pair + 2].reshape(2 * CELLS, KEYS)
            delta = jnp.sum(probs * grad_probs, axis=-1, keepdims=True)
            grad_scores = probs * (grad_probs - delta)
            b["dense"][2 * pair : 2 * pair + 2] = grad_scores.reshape(2, CELLS, KEYS)
            low = grad_scores.astype(BF16)
            packed[l, :, lanes] = (join_heads(dot(low, keys)) * scale).astype(BF16)
            grad_keys = dot(low, split_heads(b["q"][l, :, lanes]), ((0,), (0,))) * scale
            grad_values = dot(probs.astype(BF16), grads, ((0,), (0,)))
            part[:, lanes] = grad_keys[:CELLS]
            part[:, vlanes] = grad_values[:CELLS]
            out[l, :, lanes] = grad_keys[CELLS:].astype(BF16)
            out[l, :, vlanes] = grad_values[CELLS:].astype(BF16)
        for first, rows, d_lat, d_lon in SEGMENTS:
            here = pl.ds(first - 128, rows)
            to = at(lat, lon, d_lat, d_lon)
            self.copies.append(self.send(out.at[l, here], b["into"].at[l, here], to))
        self.share_packed((0,))

    def collect(self):
        b, l = self.b, self.l
        key_i = jnp.broadcast_to(b["coord"][0:1, :], (COLS, KEYS))
        step_lon = b["coord"][1:2, :] - lax.broadcasted_iota(jnp.int32, (COLS, KEYS), 0)
        ones = jnp.ones((8, KEYS), F32)
        sums, vec = b["sums"], b["vec"]
        sums[...] = jnp.zeros_like(sums)
        vec[l] = jnp.zeros((16, 128), F32)

        def step(head, _):
            for u in range(WIN):
                acc = jnp.zeros((COLS, KEYS), F32)
                for i in range(ROWS):
                    acc += jnp.where(
                        key_i == i + u - RADIUS, b["dense"][head, i * COLS : (i + 1) * COLS, :], 0.0
                    )
                for w in range(WIN):
                    o = u * WIN + w
                    sums[o : o + 1, :] = jnp.sum(
                        jnp.where(step_lon == w - RADIUS, acc, 0.0), axis=0, keepdims=True
                    )
            total = lax.dot_general(
                ones, sums[...], (((1,), (1,)), ((), ())),
                precision=lax.Precision.HIGHEST, preferred_element_type=F32,
            )
            vec[l, pl.ds(8 + head, 1), 0:56] = total[0:1]
            return 0

        lax.fori_loop(0, HEADS, step, 0)

    def backward_end(self, up, x):
        b, l = self.b, self.l
        self.wait()
        part, into, packed = b["part"], b["into"], b["packed"]
        part[80:128, :] += into[l, 0:48, :].astype(F32)
        part[0:48, :] += into[l, 48:96, :].astype(F32)
        total = part[...] + dot(b["sel"][...], into[l, 96:224, :], ((0,), (0,)))
        packed[l, :, INNER:] = total.astype(BF16)
        self.share_packed((1, 2))
        grad_normed = dot(packed[l], b["win"][l], ((1,), (1,)))
        centred, rstd = norm_parts(x)
        unit = centred * rstd
        gain_grad = jnp.sum(grad_normed * unit, axis=0, keepdims=True)
        for k in range(8):
            b["vec"][l, k : k + 1, :] = gain_grad[:, k * 128 : k * 128 + 128]
        scaled = grad_normed * b["gain"][l : l + 1, :]
        mean_a = jnp.mean(scaled, axis=-1, keepdims=True)
        mean_b = jnp.mean(scaled * unit, axis=-1, keepdims=True)
        return (up.astype(F32) + rstd * (scaled - mean_a - unit * mean_b)).astype(BF16)

    def share_early(self):
        x, y, z, core = chip()
        l, b = self.l, self.b
        to, there = device(x, y, z, 1 - core), pl.ds(CELLS, CELLS)
        self.shares = [
            self.send(b["normed"].at[l], b["nb"].at[l, there], to),
            self.send(b["mixed"].at[l], b["mb"].at[l, there], to),
            self.send(self.columns(b["up"], 1 - core, 512, 0), b["ub"].at[l, there], to),
        ]
        b["nb"][l, :CELLS] = b["normed"][l]
        b["mb"][l, :CELLS] = b["mixed"][l]
        b["ub"][l, :CELLS] = self.columns(b["up"], core, 512, 0)[...]

    def columns(self, ref, core, width, start):
        return ref.at[self.l, :, pl.ds(pl.multiple_of(core * width + start, 128), width)]

    def share_packed(self, blocks):
        x, y, z, core = chip()
        l, b = self.l, self.b
        to, there = device(x, y, z, 1 - core), pl.ds(CELLS, CELLS)
        for k in blocks:
            cols = slice(256 * k, 256 * k + 256)
            source = self.columns(b["packed"], 1 - core, 256, 512 * k)
            self.shares.append(self.send(source, b["gb"].at[l, there, pl.ds(256 * k, 256)], to))
            b["gb"][l, :CELLS, cols] = self.columns(b["packed"], core, 256, 512 * k)[...]

    def product_early(self):
        l, b = self.l, self.b
        for copy in self.shares:
            copy.wait()
        self.shares = []
        slab = b["slab"]

        def step(k, _):
            for zz in range(2):
                z = 2 * k + zz
                left = b["nb"][l, :, pl.ds(pl.multiple_of(z * 128, 128), 128)]
                term = dot(left, b["gb"][l, :, 0:256], ((0,), (0,))).astype(BF16)
                for x_low in range(2):
                    for rg in range(4):
                        for cg in range(2):
                            part, f, g = slot_of(rg // 2, 0, (rg % 2) * 2 + cg, x_low)
                            row = x_low * 64 + rg * 16
                            slab[l, part, f, g, z] = term[row : row + 16, cg * 128 : cg * 128 + 128]
            left = b["mb"][l, :, pl.ds(pl.multiple_of(k * 128, 128), 128)]
            term = dot(left, b["ub"][l], ((0,), (0,))).astype(BF16)
            for zz in range(2):
                for x_low in range(2):
                    for core in range(2):
                        for cg in range(4):
                            part, f, g = slot_of(core, 0, 4 + cg, x_low)
                            row = zz * 64 + x_low * 32 + core * 16
                            slab[l, part, f, g, 2 * k + zz] = term[
                                row : row + 16, cg * 128 : cg * 128 + 128
                            ]
            return 0

        lax.fori_loop(0, 4, step, 0)
        self.start_first(EARLY)

    def product_late(self):
        l, b = self.l, self.b
        for copy in self.shares:
            copy.wait()
        self.shares = []
        slab = b["slab"]

        def step(z, _):
            left = b["nb"][l, :, pl.ds(pl.multiple_of(z * 128, 128), 128)]
            term = dot(left, b["gb"][l, :, 256:768], ((0,), (0,))).astype(BF16)
            for x_low in range(2):
                for rg in range(4):
                    for cg in range(4):
                        part, f, g = slot_of(rg // 2, 1, (rg % 2) * 4 + cg, x_low)
                        row = x_low * 64 + rg * 16
                        slab[l, part, f, g, z] = term[row : row + 16, cg * 128 : cg * 128 + 128]
            return 0

        lax.fori_loop(0, 8, step, 0)
        self.start_first(LATE)

    def start_first(self, parts):
        l, b = self.l, self.b
        x, y, z, core = chip()
        for d in (2, 1, 3):
            for t in parts:
                f = x if X_FIRST[t] else y
                to = device(turn(x, d, 4), y, z, core) if X_FIRST[t] else device(x, turn(y, d, 4), z, core)
                self.moves[parts].append(
                    self.send(b["slab"].at[l, t, turn(f, d, 4)], b["r1"].at[l, t, d - 1], to)
                )

    def arrive(self, key):
        for copy in self.moves[key]:
            copy.wait()
        self.moves[key] = []

    def first_axis(self, parts):
        self.arrive(parts)
        l, b = self.l, self.b
        slab, r1 = b["slab"], b["r1"]
        x, y, z, core = chip()
        for t in parts:
            f = x if X_FIRST[t] else y
            total = slab[l, t, f].astype(F32)
            for k in range(3):
                total += r1[l, t, k].astype(F32)
            slab[l, t, f] = total.astype(BF16)
        for d in (2, 1, 3):
            for t in parts:
                f, g = (x, y) if X_FIRST[t] else (y, x)
                to = device(x, turn(y, d, 4), z, core) if X_FIRST[t] else device(turn(x, d, 4), y, z, core)
                self.moves[parts].append(
                    self.send(slab.at[l, t, f, turn(g, d, 4)], b["r2"].at[l, t, d - 1], to)
                )

    def second_axis(self, parts):
        self.arrive(parts)
        l, b = self.l, self.b
        slab, r2 = b["slab"], b["r2"]
        x, y, z, core = chip()
        for t in parts:
            f, g = (x, y) if X_FIRST[t] else (y, x)
            total = slab[l, t, f, g].astype(F32)
            for k in range(3):
                total += r2[l, t, k].astype(F32)
            b["zs"][l, :, t] = total.astype(BF16)

    def start_third(self):
        l, b = self.l, self.b
        x, y, z, core = chip()
        b["zr"][l, z] = b["zs"][l, z]
        for d in (4, 3, 5, 2, 6, 1, 7):
            to = turn(z, d, 8)
            self.moves["z"].append(
                self.send(b["zs"].at[l, to], b["zr"].at[l, z], device(x, y, to, core))
            )

    def third_axis(self):
        self.arrive("z")
        l, b = self.l, self.b
        x, y, z, core = chip()
        total = b["zr"][l, 0].astype(F32)
        for k in range(1, 8):
            total += b["zr"][l, k].astype(F32)
        b["fin"][l] = total.astype(BF16)
        own = 8 * core + 4 * lax.div(x, 2) + y
        b["ag"][l, own] = b["fin"][l, pl.ds(2 * core, 2)]
        for to, to_core in owners():
            self.moves["z"].append(
                self.send(b["fin"].at[l, pl.ds(2 * to_core, 2)], b["ag"].at[l, own], to)
            )

    def finish(self):
        self.arrive("z")

    def small_first(self):
        l, b = self.l, self.b
        x, y, z, core = chip()
        own = 8 * core + 4 * lax.div(x, 2) + y
        b["va"][l, own] = b["vec"][l]
        for to, _ in owners():
            self.vec_copies.append(self.send(b["vec"].at[l], b["va"].at[l, own], to))

    def small_second(self):
        l, b = self.l, self.b
        x, y, z, core = chip()
        for copy in self.vec_copies:
            copy.wait()
        total = b["va"][l, 0]
        for k in range(1, 16):
            total += b["va"][l, k]
        b["vec"][l] = total
        own = 2 * z + lax.rem(x, 2)
        b["vb"][l, own] = total
        self.vec_copies = [self.send(b["vec"].at[l], b["vb"].at[l, own], to) for to in across()]

    def small_end(self):
        l, b = self.l, self.b
        for copy in self.vec_copies:
            copy.wait()
        self.vec_copies = []
        total = b["vb"][l, 0]
        for k in range(1, 16):
            total += b["vb"][l, k]
        b["small"][l] = total


TILE = (16, 128)
INPUTS = ("x_hbm", "up_hbm", "win_hbm", "wout_hbm", "gain_hbm", "bias", "sel_hbm", "coord_hbm")
OUTPUTS = ("y_out", "down_out", "ag", "small")
SCRATCH = {
    "gain": ((LAYERS, D), F32),
    "sel": ((128, CELLS), BF16),
    "coord": ((8, KEYS), jnp.int32),
    "x": ((LAYERS, CELLS, D), BF16),
    "up": ((LAYERS, CELLS, D), BF16),
    "win": ((LAYERS, D, 3 * INNER), BF16),
    "wout": ((LAYERS, INNER, D), BF16),
    "normed": ((LAYERS, CELLS, D), BF16),
    "q": ((LAYERS, CELLS, INNER), BF16),
    "kv": ((LAYERS, KEYS, D), BF16),
    "pack": ((LAYERS, 128, D), BF16),
    "probs": ((LAYERS, HEADS, CELLS, KEYS), F32),
    "mixed": ((LAYERS, CELLS, INNER), BF16),
    "rw": ((WIN, ROWS, KEYS), F32),
    "dense": ((HEADS, CELLS, KEYS), F32),
    "gm": ((LAYERS, CELLS, INNER), BF16),
    "packed": ((LAYERS, CELLS, 3 * INNER), BF16),
    "part": ((CELLS, D), F32),
    "out": ((LAYERS, KEYS - CELLS, D), BF16),
    "into": ((LAYERS, KEYS - CELLS, D), BF16),
    "sums": ((56, KEYS), F32),
    "nb": ((LAYERS, 2 * CELLS, D), BF16),
    "mb": ((LAYERS, 2 * CELLS, INNER), BF16),
    "ub": ((LAYERS, 2 * CELLS, 512), BF16),
    "gb": ((LAYERS, 2 * CELLS, 768), BF16),
    "slab": ((LAYERS, 4, 4, 4, 8) + TILE, BF16),
    "r1": ((LAYERS, 4, 3, 4, 8) + TILE, BF16),
    "r2": ((LAYERS, 4, 3, 8) + TILE, BF16),
    "zs": ((LAYERS, 8, 4) + TILE, BF16),
    "zr": ((LAYERS, 8, 4) + TILE, BF16),
    "fin": ((LAYERS, 4) + TILE, BF16),
    "y": ((2, CELLS, D), BF16),
    "vec": ((LAYERS, 16, 128), F32),
    "va": ((LAYERS, 16, 16, 128), F32),
    "vb": ((LAYERS, 16, 16, 128), F32),
}
SENDS = 2 * (16 + 6 + 24 + 7 + 15 + 30)


def kernel(*refs):
    names = INPUTS + OUTPUTS + tuple(SCRATCH)
    b = dict(zip(names, refs))
    load_sem, send_sem, recv_sem = refs[len(names) :]
    barrier, greeted = greet()
    pairs = [(b["x_hbm"], b["x"].at[0])]
    for l in range(LAYERS):
        for cols in (pl.ds(INNER, 2 * INNER), pl.ds(0, INNER)):
            pairs.append((b["win_hbm"].at[l, :, cols], b["win"].at[l, :, cols]))
        pairs.append((b["wout_hbm"].at[l], b["wout"].at[l]))
    pairs.append((b["up_hbm"], b["up"].at[1]))
    pairs += [(b[name + "_hbm"], b[name]) for name in ("gain", "sel", "coord")]
    loads = [pltpu.make_async_copy(src, dst, load_sem.at[n]) for n, (src, dst) in enumerate(pairs)]
    for n in (0, 8, 1, 9, 2, 10, 3, 7, 4, 5, 6):
        loads[n].start()
    send = Sender(send_sem, recv_sem)
    first = Layer(0, b, send, loads[1:4])
    second = Layer(1, b, send, loads[4:7])
    for n in (0, 8, 9, 10):
        loads[n].wait()
    x = b["x"][0].astype(F32)
    first.forward_start(x, lambda: pl.semaphore_wait(barrier, greeted))
    b["x"][1] = first.forward_end(x)
    x = b["x"][1].astype(F32)
    second.forward_start(x, lambda: None)
    loads[7].wait()
    second.load(2)
    second.mixed_grad(b["up"][1])
    b["y"][0] = second.forward_end(x)
    saves = [pltpu.make_async_copy(b["y"].at[0], b["y_out"], load_sem.at[11])]
    saves[0].start()
    second.share_early()
    second.backward_start()
    second.product_early()
    second.collect()
    b["up"][0] = second.backward_end(b["up"][1], b["x"][1].astype(F32))
    up = b["up"][0]
    first.mixed_grad(up)
    first.share_early()
    second.product_late()
    second.small_first()
    first.backward_start()
    first.product_early()
    second.first_axis(EARLY)
    first.collect()
    second.first_axis(LATE)
    second.small_second()
    b["y"][1] = first.backward_end(up, b["x"][0].astype(F32))
    saves.append(pltpu.make_async_copy(b["y"].at[1], b["down_out"], load_sem.at[12]))
    saves[1].start()
    first.product_late()
    first.small_first()
    second.second_axis(EARLY)
    second.second_axis(LATE)
    second.start_third()
    first.first_axis(EARLY)
    second.third_axis()
    second.small_end()
    first.first_axis(LATE)
    first.small_second()
    first.second_axis(EARLY)
    second.finish()
    first.second_axis(LATE)
    first.start_third()
    first.small_end()
    first.third_axis()
    first.finish()
    for save in saves:
        save.wait()


def lay_out(y_ref, down_ref, ag, small, y_out, down_out, in_out, out_out, gain_out, bias_out):
    y_out[...] = y_ref[...]
    down_out[...] = down_ref[...]
    for l in range(LAYERS):
        for slot in range(16):
            core_of, index = slot // 8, slot % 8
            early, late = ag[l, slot, 0].astype(F32), ag[l, slot, 1].astype(F32)
            if index < 4:
                row, col = 16 * (index // 2), 256 * core_of + 128 * (index % 2)
                in_out[l, row : row + 16, col : col + 128] = early
            else:
                col = core_of * 512 + (index - 4) * 128
                out_out[l, :, col : col + 128] = early
            row = 16 * (index // 4)
            col = 512 * (1 + (index % 4) // 2) + 256 * core_of + 128 * (index % 2)
            in_out[l, row : row + 16, col : col + 128] = late
        for k in range(8):
            gain_out[l : l + 1, k * 128 : k * 128 + 128] = small[l, k : k + 1, :]
        bias_out[l] = small[l, 8:16, : WIN * WIN]


def solution_step(inputs, input_weight, output_weight, norm_gain, position_bias, cotangent):
    whole, far = pl.BlockSpec(memory_space=pltpu.VMEM), pl.BlockSpec(memory_space=pl.ANY)
    scalars = pl.BlockSpec(memory_space=pltpu.SMEM)
    shape = jax.ShapeDtypeStruct
    results = pl.pallas_call(
        kernel,
        out_shape=(
            shape((CELLS, D), BF16),
            shape((CELLS, D), BF16),
            shape((LAYERS, 16, 2) + TILE, BF16),
            shape((LAYERS, 16, 128), F32),
        ),
        in_specs=[far] * 5 + [scalars, far, far],
        out_specs=(far, far, whole, whole),
        scratch_shapes=[pltpu.VMEM(*spec) for spec in SCRATCH.values()]
        + [
            pltpu.SemaphoreType.DMA((13,)),
            pltpu.SemaphoreType.DMA((SENDS,)),
            pltpu.SemaphoreType.DMA((SENDS,)),
        ],
        compiler_params=pltpu.CompilerParams(
            collective_id=0, has_side_effects=True, vmem_limit_bytes=60 * 1024 * 1024
        ),
    )(
        inputs.reshape(CELLS, D),
        cotangent.reshape(CELLS, D),
        input_weight,
        output_weight,
        norm_gain,
        position_bias,
        jnp.asarray(SELECT, BF16),
        jnp.asarray(KEY_COORD),
    )
    y, down, in_grad, out_grad, gain_grad, bias_grad = pl.pallas_call(
        lay_out,
        out_shape=(
            shape((CELLS, D), BF16),
            shape((CELLS, D), BF16),
            shape((LAYERS, 32, 1536), F32),
            shape((LAYERS, 16, 1024), F32),
            shape((LAYERS, D), F32),
            shape((LAYERS, HEADS, WIN * WIN), F32),
        ),
        in_specs=[whole] * 4,
        out_specs=(whole,) * 6,
    )(*results)
    tile = (ROWS, COLS, D)
    return y.reshape(tile), down.reshape(tile), in_grad, out_grad, gain_grad, bias_grad


def solution(mesh):
    return jax.shard_map(
        solution_step,
        mesh=mesh,
        in_specs=(P("lat", "lon", None), P(), P(), P(), P(), P("lat", "lon", None)),
        out_specs=(
            P("lat", "lon", None),
            P("lat", "lon", None),
            P(None, "lon", None),
            P(None, "lon", None),
            P(),
            P(),
        ),
        check_vma=False,
    )
```

```python
import jax
import jax.numpy as jnp
import numpy as np
from jax import lax
from jax.experimental import pallas as pl
from jax.experimental.pallas import tpu as pltpu
from jax.sharding import PartitionSpec as P

HEADS = 8
HEAD_DIM = 64
WIN = 7
RADIUS = 3
LAYERS = 2
D = 1024
INNER = 512
ROWS, COLS = 8, 16
CELLS = ROWS * COLS
KEYS = 352
EPS = 1e-05
MESH = pl.DeviceIdType.MESH
F32, BF16 = jnp.float32, jnp.bfloat16

SEGMENTS = (
    (128, 48, -1, 0),
    (176, 48, 1, 0),
    (224, 32, 0, -1),
    (256, 32, 0, 1),
    (288, 16, -1, -1),
    (304, 16, -1, 1),
    (320, 16, 1, -1),
    (336, 16, 1, 1),
)


def geometry():
    key_coord = np.full((8, KEYS), 1000, np.int32)
    select = np.zeros((128, CELLS), np.float32)
    for i in range(ROWS):
        for j in range(COLS):
            key_coord[0, i * COLS + j], key_coord[1, i * COLS + j] = i, j
    for first, _, d_lat, d_lon in SEGMENTS:
        rows = {-1: range(5, 8), 0: range(8), 1: range(3)}[d_lat]
        cols = {-1: range(13, 16), 0: range(16), 1: range(3)}[d_lon]
        place = first
        for i in rows:
            for j in cols:
                key_coord[0, place], key_coord[1, place] = i + d_lat * ROWS, j + d_lon * COLS
                if d_lon != 0:
                    select[place - 224, i * COLS + j] = 1.0
                place += 1
    return key_coord, select


KEY_COORD, SELECT = geometry()


def place():
    return lax.axis_index("lat"), lax.axis_index("lon")


def at(lat, lon, d_lat, d_lon):
    return (lax.rem(lat + d_lat + 8, 8), lax.rem(lon + d_lon + 32, 32))


def dot(a, b, dims=((1,), (0,))):
    return lax.dot_general(a, b, (dims, ((), ())), preferred_element_type=F32)


def norm_parts(x):
    mean = jnp.mean(x, axis=-1, keepdims=True)
    centred = x - mean
    var = jnp.mean(centred * centred, axis=-1, keepdims=True)
    return centred, lax.rsqrt(var + EPS)


def split_heads(pair):
    low = lax.broadcasted_iota(jnp.int32, pair.shape, 1) < HEAD_DIM
    zero = jnp.zeros_like(pair)
    return jnp.concatenate([jnp.where(low, pair, zero), jnp.where(low, zero, pair)], axis=0)


def join_heads(both):
    low = lax.broadcasted_iota(jnp.int32, (CELLS, 2 * HEAD_DIM), 1) < HEAD_DIM
    return jnp.where(low, both[:CELLS], both[CELLS:])


def chip():
    lat, lon = place()
    x = 2 * lax.rem(lat, 2) + lax.rem(lax.div(lon, 2), 2)
    return x, lax.div(lat, 2), lax.div(lon, 4), lax.rem(lon, 2)


def device(x, y, z, core):
    return (2 * y + lax.div(x, 2), 4 * z + 2 * lax.rem(x, 2) + core)


def turn(index, step, count):
    return lax.rem(index + step, count)


def owners():
    x, y, z, core = chip()
    x_high, x_low = lax.div(x, 2), lax.rem(x, 2)
    for d in range(1, 16):
        to_core = 1 - core if d // 8 else core
        to_high = 1 - x_high if (d // 4) % 2 else x_high
        yield device(2 * to_high + x_low, turn(y, d % 4, 4), z, to_core), to_core


def across():
    x, y, z, core = chip()
    x_high, x_low = lax.div(x, 2), lax.rem(x, 2)
    for d in range(1, 16):
        to_low = 1 - x_low if d % 2 else x_low
        yield device(2 * x_high + to_low, y, turn(z, d // 2, 8), core)


def greet():
    lat, lon = place()
    x, y, z, core = chip()
    peers = [to for to, _ in owners()] + list(across()) + [device(3 - x, y, z, core)]
    peers += [at(lat, lon, d_lat, d_lon) for _, _, d_lat, d_lon in SEGMENTS if d_lon != 0]
    barrier = pltpu.get_barrier_semaphore()
    for to in peers:
        pl.semaphore_signal(barrier, inc=1, device_id=to, device_id_type=MESH)
    return barrier, len(peers)


X_FIRST = (True, False, False, True)
EARLY, LATE = (0, 2), (1, 3)


def slot_of(core, late, index, x_low):
    part = 2 * core + late
    x, y = 2 * (index // 4) + x_low, index % 4
    return (part, x, y) if X_FIRST[part] else (part, y, x)


class Sender:
    def __init__(self, send_sem, recv_sem):
        self.send_sem, self.recv_sem, self.count = send_sem, recv_sem, 0

    def __call__(self, src, dst, to):
        copy = pltpu.make_async_remote_copy(
            src_ref=src,
            dst_ref=dst,
            send_sem=self.send_sem.at[self.count],
            recv_sem=self.recv_sem.at[self.count],
            device_id=to,
            device_id_type=MESH,
        )
        copy.start()
        self.count += 1
        return copy


class Layer:
    def __init__(self, l, b, send, loads):
        self.l, self.b, self.send, self.loads = l, b, send, loads
        self.copies, self.vec_copies, self.pending = [], [], [0, 1, 2, 3]
        self.late_copies = []
        self.shares, self.moves = [], {EARLY: [], LATE: [], "z": []}

    def load(self, n):
        if n in self.pending:
            self.pending.remove(n)
            self.loads[n].wait()

    def forward_start(self, x, before_send):
        b, l = self.b, self.l
        lat, lon = place()
        centred, rstd = norm_parts(x)
        normed = (centred * rstd * b["gain"][l : l + 1, :]).astype(BF16)
        b["normed"][l] = normed
        for n, which in enumerate((0, 3)):
            self.load(which)
            lanes = slice(INNER * n, INNER * n + INNER)
            block = dot(normed, b["win"][l, :, INNER + INNER * n : 2 * INNER + INNER * n]).astype(BF16)
            b["kv"][l, 0:CELLS, lanes] = block
            b["pack"][l, :, lanes] = dot(b["sel"][...], block).astype(BF16)
            if n == 0:
                before_send()
            lanes = pl.ds(INNER * n, INNER)
            for first, rows, d_lat, d_lon in SEGMENTS:
                if d_lon == 0:
                    source = b["kv"].at[l, pl.ds(80 if d_lat < 0 else 0, rows), lanes]
                else:
                    source = b["pack"].at[l, pl.ds(first - 224, rows), lanes]
                to = at(lat, lon, -d_lat, -d_lon)
                move = self.send(source, b["kv"].at[l, pl.ds(first, rows), lanes], to)
                (self.late_copies if n else self.copies).append(move)
        self.load(1)
        b["q"][l] = dot(normed, b["win"][l, :, :INNER]).astype(BF16)
        self.expand()

    def expand(self):
        b, l = self.b, self.l
        lat, lon = place()
        key_i = b["coord"][0:1, :]
        row_ok = (lat * ROWS + key_i >= 0) & (lat * ROWS + key_i < 64)
        step_lat = jnp.where(row_ok, key_i, 1000) - lax.broadcasted_iota(jnp.int32, (ROWS, KEYS), 0)
        step_lon = b["coord"][1:2, :] - lax.broadcasted_iota(jnp.int32, (COLS, KEYS), 0)
        bias, rw, dense = b["bias"], b["rw"], b["dense"]

        def step(head, _):
            for w in range(WIN):
                acc = jnp.full((ROWS, KEYS), -jnp.inf, F32)
                for u in range(WIN):
                    acc = jnp.where(step_lat == u - RADIUS, bias[l, head, u * WIN + w], acc)
                rw[w] = acc
            for i in range(ROWS):
                acc = jnp.full((COLS, KEYS), -jnp.inf, F32)
                for w in range(WIN):
                    acc = jnp.where(step_lon == w - RADIUS, rw[w, i : i + 1, :], acc)
                dense[head, i * COLS : (i + 1) * COLS, :] = acc
            return 0

        lax.fori_loop(0, HEADS, step, 0)

    def wait(self):
        for copy in self.copies:
            copy.wait()
        self.copies = []

    def forward_end(self, x):
        b, l = self.b, self.l
        self.wait()
        kv = b["kv"]
        for pair in range(HEADS // 2):
            lanes = slice(pair * 128, pair * 128 + 128)
            queries = split_heads(b["q"][l, :, lanes])
            bias = b["dense"][2 * pair : 2 * pair + 2].reshape(2 * CELLS, KEYS)
            scores = dot(queries, kv[l, :, lanes], ((1,), (1,))) * HEAD_DIM ** (-0.5) + bias
            top = jnp.max(scores, axis=-1, keepdims=True)
            weight = jnp.exp(scores - top)
            probs = weight / jnp.sum(weight, axis=-1, keepdims=True)
            b["probs"][l, 2 * pair : 2 * pair + 2] = probs.reshape(2, CELLS, KEYS)
        self.copies, self.late_copies = self.late_copies, []
        self.wait()
        for pair in range(HEADS // 2):
            lanes = slice(pair * 128, pair * 128 + 128)
            probs = b["probs"][l, 2 * pair : 2 * pair + 2].reshape(2 * CELLS, KEYS)
            values = kv[l, :, INNER + pair * 128 : INNER + pair * 128 + 128]
            b["mixed"][l, :, lanes] = join_heads(dot(probs.astype(BF16), values)).astype(BF16)
        self.load(2)
        return (x + dot(b["mixed"][l], b["wout"][l])).astype(BF16)

    def mixed_grad(self, up):
        self.b["gm"][self.l] = dot(up, self.b["wout"][self.l], ((1,), (1,))).astype(BF16)

    def backward_start(self):
        b, l = self.b, self.l
        lat, lon = place()
        scale = HEAD_DIM ** (-0.5)
        kv, packed, part, out = b["kv"], b["packed"], b["part"], b["out"]
        for pair in range(HEADS // 2):
            lanes = slice(pair * 128, pair * 128 + 128)
            vlanes = slice(INNER + pair * 128, INNER + pair * 128 + 128)
            keys = kv[l, :, lanes]
            grads = split_heads(b["gm"][l, :, lanes])
            grad_probs = dot(grads, kv[l, :, vlanes], ((1,), (1,)))
            probs = b["probs"][l, 2 * pair : 2 * pair + 2].reshape(2 * CELLS, KEYS)
            delta = jnp.sum(probs * grad_probs, axis=-1, keepdims=True)
            grad_scores = probs * (grad_probs - delta)
            b["dense"][2 * pair : 2 * pair + 2] = grad_scores.reshape(2, CELLS, KEYS)
            low = grad_scores.astype(BF16)
            packed[l, :, lanes] = (join_heads(dot(low, keys)) * scale).astype(BF16)
            grad_keys = dot(low, split_heads(b["q"][l, :, lanes]), ((0,), (0,))) * scale
            grad_values = dot(probs.astype(BF16), grads, ((0,), (0,)))
            half, k = pair // 2, 128 * (pair % 2)
            part[half, :, k : k + 128] = grad_keys[:CELLS]
            part[half, :, 256 + k : 384 + k] = grad_values[:CELLS]
            out[l, half, :, k : k + 128] = grad_keys[CELLS:].astype(BF16)
            out[l, half, :, 256 + k : 384 + k] = grad_values[CELLS:].astype(BF16)
            if k:
                for first, rows, d_lat, d_lon in SEGMENTS:
                    here = pl.ds(first - 128, rows)
                    to = at(lat, lon, d_lat, d_lon)
                    move = self.send(out.at[l, half, here], b["into"].at[l, half, here], to)
                    self.copies.append(move)
        self.share_packed((0,))

    def collect(self):
        b, l = self.b, self.l
        key_i = jnp.broadcast_to(b["coord"][0:1, :], (COLS, KEYS))
        step_lon = b["coord"][1:2, :] - lax.broadcasted_iota(jnp.int32, (COLS, KEYS), 0)
        ones = jnp.ones((8, KEYS), F32)
        sums, vec = b["sums"], b["vec"]
        sums[...] = jnp.zeros_like(sums)
        vec[l] = jnp.zeros((16, 128), F32)

        def step(head, _):
            for u in range(WIN):
                acc = jnp.zeros((COLS, KEYS), F32)
                for i in range(ROWS):
                    acc += jnp.where(
                        key_i == i + u - RADIUS, b["dense"][head, i * COLS : (i + 1) * COLS, :], 0.0
                    )
                for w in range(WIN):
                    o = u * WIN + w
                    sums[o : o + 1, :] = jnp.sum(
                        jnp.where(step_lon == w - RADIUS, acc, 0.0), axis=0, keepdims=True
                    )
            total = lax.dot_general(
                ones, sums[...], (((1,), (1,)), ((), ())),
                precision=lax.Precision.HIGHEST, preferred_element_type=F32,
            )
            vec[l, pl.ds(8 + head, 1), 0:56] = total[0:1]
            return 0

        lax.fori_loop(0, HEADS, step, 0)

    def backward_end(self, up, x):
        b, l = self.b, self.l
        self.wait()
        part, into, packed = b["part"], b["into"], b["packed"]
        for half in range(2):
            part[half, 80:128, :] += into[l, half, 0:48, :].astype(F32)
            part[half, 0:48, :] += into[l, half, 48:96, :].astype(F32)
            total = part[half] + dot(b["sel"][...], into[l, half, 96:224, :], ((0,), (0,)))
            packed[l, :, INNER + 256 * half : INNER + 256 * half + 256] = total[:, :256].astype(BF16)
            packed[l, :, 2 * INNER + 256 * half : 2 * INNER + 256 * half + 256] = total[:, 256:].astype(BF16)
        self.share_packed((1, 2))
        grad_normed = dot(packed[l], b["win"][l], ((1,), (1,)))
        centred, rstd = norm_parts(x)
        unit = centred * rstd
        gain_grad = jnp.sum(grad_normed * unit, axis=0, keepdims=True)
        for k in range(8):
            b["vec"][l, k : k + 1, :] = gain_grad[:, k * 128 : k * 128 + 128]
        scaled = grad_normed * b["gain"][l : l + 1, :]
        mean_a = jnp.mean(scaled, axis=-1, keepdims=True)
        mean_b = jnp.mean(scaled * unit, axis=-1, keepdims=True)
        return (up.astype(F32) + rstd * (scaled - mean_a - unit * mean_b)).astype(BF16)

    def share_early(self):
        x, y, z, core = chip()
        l, b = self.l, self.b
        to, there = device(x, y, z, 1 - core), pl.ds(CELLS, CELLS)
        self.shares = [
            self.send(b["normed"].at[l], b["nb"].at[l, there], to),
            self.send(b["mixed"].at[l], b["mb"].at[l, there], to),
            self.send(self.columns(b["up"], 1 - core, 512, 0), b["ub"].at[l, there], to),
        ]
        b["nb"][l, :CELLS] = b["normed"][l]
        b["mb"][l, :CELLS] = b["mixed"][l]
        b["ub"][l, :CELLS] = self.columns(b["up"], core, 512, 0)[...]

    def columns(self, ref, core, width, start):
        return ref.at[self.l, :, pl.ds(pl.multiple_of(core * width + start, 128), width)]

    def share_packed(self, blocks):
        x, y, z, core = chip()
        l, b = self.l, self.b
        to, there = device(x, y, z, 1 - core), pl.ds(CELLS, CELLS)
        for k in blocks:
            cols = slice(256 * k, 256 * k + 256)
            source = self.columns(b["packed"], 1 - core, 256, 512 * k)
            self.shares.append(self.send(source, b["gb"].at[l, there, pl.ds(256 * k, 256)], to))
            b["gb"][l, :CELLS, cols] = self.columns(b["packed"], core, 256, 512 * k)[...]

    def product_early(self):
        l, b = self.l, self.b
        for copy in self.shares:
            copy.wait()
        self.shares = []
        slab = b["slab"]

        def step(k, _):
            for zz in range(2):
                z = 2 * k + zz
                left = b["nb"][l, :, pl.ds(pl.multiple_of(z * 128, 128), 128)]
                term = dot(left, b["gb"][l, :, 0:256], ((0,), (0,))).astype(BF16)
                for x_low in range(2):
                    for rg in range(4):
                        for cg in range(2):
                            part, f, g = slot_of(rg // 2, 0, (rg % 2) * 2 + cg, x_low)
                            row = x_low * 64 + rg * 16
                            slab[l, part, f, g, z] = term[row : row + 16, cg * 128 : cg * 128 + 128]
            left = b["mb"][l, :, pl.ds(pl.multiple_of(k * 128, 128), 128)]
            term = dot(left, b["ub"][l], ((0,), (0,))).astype(BF16)
            for zz in range(2):
                for x_low in range(2):
                    for core in range(2):
                        for cg in range(4):
                            part, f, g = slot_of(core, 0, 4 + cg, x_low)
                            row = zz * 64 + x_low * 32 + core * 16
                            slab[l, part, f, g, 2 * k + zz] = term[
                                row : row + 16, cg * 128 : cg * 128 + 128
                            ]
            return 0

        lax.fori_loop(0, 4, step, 0)
        self.start_first(EARLY)

    def product_late(self):
        l, b = self.l, self.b
        for copy in self.shares:
            copy.wait()
        self.shares = []
        slab = b["slab"]

        def step(z, _):
            left = b["nb"][l, :, pl.ds(pl.multiple_of(z * 128, 128), 128)]
            term = dot(left, b["gb"][l, :, 256:768], ((0,), (0,))).astype(BF16)
            for x_low in range(2):
                for rg in range(4):
                    for cg in range(4):
                        part, f, g = slot_of(rg // 2, 1, (rg % 2) * 4 + cg, x_low)
                        row = x_low * 64 + rg * 16
                        slab[l, part, f, g, z] = term[row : row + 16, cg * 128 : cg * 128 + 128]
            return 0

        lax.fori_loop(0, 8, step, 0)
        self.start_first(LATE)

    def start_first(self, parts):
        l, b = self.l, self.b
        x, y, z, core = chip()
        for d in (2, 1, 3):
            for t in parts:
                f = x if X_FIRST[t] else y
                to = device(turn(x, d, 4), y, z, core) if X_FIRST[t] else device(x, turn(y, d, 4), z, core)
                self.moves[parts].append(
                    self.send(b["slab"].at[l, t, turn(f, d, 4)], b["r1"].at[l, t, d - 1], to)
                )

    def arrive(self, key):
        for copy in self.moves[key]:
            copy.wait()
        self.moves[key] = []

    def first_axis(self, parts):
        self.arrive(parts)
        l, b = self.l, self.b
        slab, r1 = b["slab"], b["r1"]
        x, y, z, core = chip()
        for t in parts:
            f = x if X_FIRST[t] else y
            total = slab[l, t, f].astype(F32)
            for k in range(3):
                total += r1[l, t, k].astype(F32)
            slab[l, t, f] = total.astype(BF16)
        for d in (2, 1, 3):
            for t in parts:
                f, g = (x, y) if X_FIRST[t] else (y, x)
                to = device(x, turn(y, d, 4), z, core) if X_FIRST[t] else device(turn(x, d, 4), y, z, core)
                self.moves[parts].append(
                    self.send(slab.at[l, t, f, turn(g, d, 4)], b["r2"].at[l, t, d - 1], to)
                )

    def second_axis(self, parts):
        self.arrive(parts)
        l, b = self.l, self.b
        slab, r2 = b["slab"], b["r2"]
        x, y, z, core = chip()
        for t in parts:
            f, g = (x, y) if X_FIRST[t] else (y, x)
            total = slab[l, t, f, g].astype(F32)
            for k in range(3):
                total += r2[l, t, k].astype(F32)
            b["zs"][l, :, t] = total.astype(BF16)

    def start_third(self):
        l, b = self.l, self.b
        x, y, z, core = chip()
        b["zr"][l, z] = b["zs"][l, z]
        for d in (4, 3, 5, 2, 6, 1, 7):
            to = turn(z, d, 8)
            self.moves["z"].append(
                self.send(b["zs"].at[l, to], b["zr"].at[l, z], device(x, y, to, core))
            )

    def third_axis(self):
        self.arrive("z")
        l, b = self.l, self.b
        x, y, z, core = chip()
        total = b["zr"][l, 0].astype(F32)
        for k in range(1, 8):
            total += b["zr"][l, k].astype(F32)
        b["fin"][l] = total.astype(BF16)
        own = 8 * core + 4 * lax.div(x, 2) + y
        b["ag"][l, own] = b["fin"][l, pl.ds(2 * core, 2)]
        for to, to_core in owners():
            self.moves["z"].append(
                self.send(b["fin"].at[l, pl.ds(2 * to_core, 2)], b["ag"].at[l, own], to)
            )

    def finish(self):
        self.arrive("z")

    def small_first(self):
        l, b = self.l, self.b
        x, y, z, core = chip()
        own = 8 * core + 4 * lax.div(x, 2) + y
        b["va"][l, own] = b["vec"][l]
        for to, _ in owners():
            self.vec_copies.append(self.send(b["vec"].at[l], b["va"].at[l, own], to))

    def small_second(self):
        l, b = self.l, self.b
        x, y, z, core = chip()
        for copy in self.vec_copies:
            copy.wait()
        total = b["va"][l, 0]
        for k in range(1, 16):
            total += b["va"][l, k]
        b["vec"][l] = total
        own = 2 * z + lax.rem(x, 2)
        b["vb"][l, own] = total
        self.vec_copies = [self.send(b["vec"].at[l], b["vb"].at[l, own], to) for to in across()]

    def small_end(self):
        l, b = self.l, self.b
        for copy in self.vec_copies:
            copy.wait()
        self.vec_copies = []
        total = b["vb"][l, 0]
        for k in range(1, 16):
            total += b["vb"][l, k]
        b["small"][l] = total


TILE = (16, 128)
INPUTS = ("x_hbm", "up_hbm", "win_hbm", "wout_hbm", "gain_hbm", "bias", "sel_hbm", "coord_hbm")
OUTPUTS = ("y_out", "down_out", "ag", "small")
SCRATCH = {
    "gain": ((LAYERS, D), F32),
    "sel": ((128, CELLS), BF16),
    "coord": ((8, KEYS), jnp.int32),
    "x": ((LAYERS, CELLS, D), BF16),
    "up": ((LAYERS, CELLS, D), BF16),
    "win": ((LAYERS, D, 3 * INNER), BF16),
    "wout": ((LAYERS, INNER, D), BF16),
    "normed": ((LAYERS, CELLS, D), BF16),
    "q": ((LAYERS, CELLS, INNER), BF16),
    "kv": ((LAYERS, KEYS, D), BF16),
    "pack": ((LAYERS, 128, D), BF16),
    "probs": ((LAYERS, HEADS, CELLS, KEYS), F32),
    "mixed": ((LAYERS, CELLS, INNER), BF16),
    "rw": ((WIN, ROWS, KEYS), F32),
    "dense": ((HEADS, CELLS, KEYS), F32),
    "gm": ((LAYERS, CELLS, INNER), BF16),
    "packed": ((LAYERS, CELLS, 3 * INNER), BF16),
    "part": ((2, CELLS, 512), F32),
    "out": ((LAYERS, 2, KEYS - CELLS, 512), BF16),
    "into": ((LAYERS, 2, KEYS - CELLS, 512), BF16),
    "sums": ((56, KEYS), F32),
    "nb": ((LAYERS, 2 * CELLS, D), BF16),
    "mb": ((LAYERS, 2 * CELLS, INNER), BF16),
    "ub": ((LAYERS, 2 * CELLS, 512), BF16),
    "gb": ((LAYERS, 2 * CELLS, 768), BF16),
    "slab": ((LAYERS, 4, 4, 4, 8) + TILE, BF16),
    "r1": ((LAYERS, 4, 3, 4, 8) + TILE, BF16),
    "r2": ((LAYERS, 4, 3, 8) + TILE, BF16),
    "zs": ((LAYERS, 8, 4) + TILE, BF16),
    "zr": ((LAYERS, 8, 4) + TILE, BF16),
    "fin": ((LAYERS, 4) + TILE, BF16),
    "y": ((2, CELLS, D), BF16),
    "vec": ((LAYERS, 16, 128), F32),
    "va": ((LAYERS, 16, 16, 128), F32),
    "vb": ((LAYERS, 16, 16, 128), F32),
}
SENDS = 2 * (32 + 6 + 24 + 7 + 15 + 30)


def kernel(*refs):
    names = INPUTS + OUTPUTS + tuple(SCRATCH)
    b = dict(zip(names, refs))
    load_sem, send_sem, recv_sem = refs[len(names) :]
    barrier, greeted = greet()
    pairs = [(b["x_hbm"], b["x"].at[0])]
    key_cols, value_cols, query_cols = pl.ds(INNER, INNER), pl.ds(2 * INNER, INNER), pl.ds(0, INNER)
    for l in range(LAYERS):
        for cols in (key_cols, query_cols):
            pairs.append((b["win_hbm"].at[l, :, cols], b["win"].at[l, :, cols]))
        pairs.append((b["wout_hbm"].at[l], b["wout"].at[l]))
    pairs.append((b["up_hbm"], b["up"].at[1]))
    pairs += [(b[name + "_hbm"], b[name]) for name in ("gain", "sel", "coord")]
    pairs += [(b["win_hbm"].at[l, :, value_cols], b["win"].at[l, :, value_cols]) for l in range(LAYERS)]
    loads = [pltpu.make_async_copy(src, dst, load_sem.at[n]) for n, (src, dst) in enumerate(pairs)]
    for n in (0, 8, 1, 11, 9, 10):
        loads[n].start()
    send = Sender(send_sem, recv_sem)
    first = Layer(0, b, send, loads[1:4] + loads[11:12])
    second = Layer(1, b, send, loads[4:7] + loads[12:13])
    for n in (0, 8, 9, 10):
        loads[n].wait()
    x = b["x"][0].astype(F32)

    def begin():
        for n in (2, 3, 4, 12, 5, 7, 6):
            loads[n].start()
        pl.semaphore_wait(barrier, greeted)

    first.forward_start(x, begin)
    b["x"][1] = first.forward_end(x)
    x = b["x"][1].astype(F32)
    second.forward_start(x, lambda: None)
    loads[7].wait()
    second.load(2)
    second.mixed_grad(b["up"][1])
    b["y"][0] = second.forward_end(x)
    saves = [pltpu.make_async_copy(b["y"].at[0], b["y_out"], load_sem.at[13])]
    saves[0].start()
    second.share_early()
    second.backward_start()
    second.product_early()
    second.collect()
    b["up"][0] = second.backward_end(b["up"][1], b["x"][1].astype(F32))
    up = b["up"][0]
    first.mixed_grad(up)
    first.share_early()
    second.small_first()
    second.first_axis(EARLY)
    first.backward_start()
    second.product_late()
    first.product_early()
    first.collect()
    second.first_axis(LATE)
    second.small_second()
    b["y"][1] = first.backward_end(up, b["x"][0].astype(F32))
    saves.append(pltpu.make_async_copy(b["y"].at[1], b["down_out"], load_sem.at[14]))
    saves[1].start()
    first.product_late()
    first.small_first()
    second.second_axis(EARLY)
    second.second_axis(LATE)
    second.start_third()
    first.first_axis(EARLY)
    second.third_axis()
    second.small_end()
    first.first_axis(LATE)
    first.small_second()
    first.second_axis(EARLY)
    second.finish()
    first.second_axis(LATE)
    first.start_third()
    first.small_end()
    first.third_axis()
    first.finish()
    for save in saves:
        save.wait()


def lay_out(y_ref, down_ref, ag, small, y_out, down_out, in_out, out_out, gain_out, bias_out):
    y_out[...] = y_ref[...]
    down_out[...] = down_ref[...]
    for l in range(LAYERS):
        for slot in range(16):
            core_of, index = slot // 8, slot % 8
            early, late = ag[l, slot, 0].astype(F32), ag[l, slot, 1].astype(F32)
            if index < 4:
                row, col = 16 * (index // 2), 256 * core_of + 128 * (index % 2)
                in_out[l, row : row + 16, col : col + 128] = early
            else:
                col = core_of * 512 + (index - 4) * 128
                out_out[l, :, col : col + 128] = early
            row = 16 * (index // 4)
            col = 512 * (1 + (index % 4) // 2) + 256 * core_of + 128 * (index % 2)
            in_out[l, row : row + 16, col : col + 128] = late
        for k in range(8):
            gain_out[l : l + 1, k * 128 : k * 128 + 128] = small[l, k : k + 1, :]
        bias_out[l] = small[l, 8:16, : WIN * WIN]


def solution_step(inputs, input_weight, output_weight, norm_gain, position_bias, cotangent):
    whole, far = pl.BlockSpec(memory_space=pltpu.VMEM), pl.BlockSpec(memory_space=pl.ANY)
    scalars = pl.BlockSpec(memory_space=pltpu.SMEM)
    shape = jax.ShapeDtypeStruct
    results = pl.pallas_call(
        kernel,
        out_shape=(
            shape((CELLS, D), BF16),
            shape((CELLS, D), BF16),
            shape((LAYERS, 16, 2) + TILE, BF16),
            shape((LAYERS, 16, 128), F32),
        ),
        in_specs=[far] * 5 + [scalars, far, far],
        out_specs=(far, far, whole, whole),
        scratch_shapes=[pltpu.VMEM(*spec) for spec in SCRATCH.values()]
        + [
            pltpu.SemaphoreType.DMA((15,)),
            pltpu.SemaphoreType.DMA((SENDS,)),
            pltpu.SemaphoreType.DMA((SENDS,)),
        ],
        compiler_params=pltpu.CompilerParams(
            collective_id=0, has_side_effects=True, vmem_limit_bytes=60 * 1024 * 1024
        ),
    )(
        inputs.reshape(CELLS, D),
        cotangent.reshape(CELLS, D),
        input_weight,
        output_weight,
        norm_gain,
        position_bias,
        jnp.asarray(SELECT, BF16),
        jnp.asarray(KEY_COORD),
    )
    y, down, in_grad, out_grad, gain_grad, bias_grad = pl.pallas_call(
        lay_out,
        out_shape=(
            shape((CELLS, D), BF16),
            shape((CELLS, D), BF16),
            shape((LAYERS, 32, 1536), F32),
            shape((LAYERS, 16, 1024), F32),
            shape((LAYERS, D), F32),
            shape((LAYERS, HEADS, WIN * WIN), F32),
        ),
        in_specs=[whole] * 4,
        out_specs=(whole,) * 6,
    )(*results)
    tile = (ROWS, COLS, D)
    return y.reshape(tile), down.reshape(tile), in_grad, out_grad, gain_grad, bias_grad


def solution(mesh):
    return jax.shard_map(
        solution_step,
        mesh=mesh,
        in_specs=(P("lat", "lon", None), P(), P(), P(), P(), P("lat", "lon", None)),
        out_specs=(
            P("lat", "lon", None),
            P("lat", "lon", None),
            P(None, "lon", None),
            P(None, "lon", None),
            P(),
            P(),
        ),
        check_vma=False,
    )
```

```python
import jax
import jax.numpy as jnp
import numpy as np
from jax import lax
from jax.experimental import pallas as pl
from jax.experimental.pallas import tpu as pltpu
from jax.sharding import PartitionSpec as P

HEADS = 8
HEAD_DIM = 64
WIN = 7
RADIUS = 3
LAYERS = 2
D = 1024
INNER = 512
ROWS, COLS = 8, 16
CELLS = ROWS * COLS
KEYS = 352
EPS = 1e-05
MESH = pl.DeviceIdType.MESH
F32, BF16 = jnp.float32, jnp.bfloat16

SEGMENTS = (
    (128, 48, -1, 0),
    (176, 48, 1, 0),
    (288, 16, -1, -1),
    (304, 16, -1, 1),
    (320, 16, 1, -1),
    (336, 16, 1, 1),
    (224, 32, 0, -1),
    (256, 32, 0, 1),
)


def geometry():
    key_coord = np.full((8, KEYS), 1000, np.int32)
    select = np.zeros((128, CELLS), np.float32)
    for i in range(ROWS):
        for j in range(COLS):
            key_coord[0, i * COLS + j], key_coord[1, i * COLS + j] = i, j
    for first, _, d_lat, d_lon in SEGMENTS:
        rows = {-1: range(5, 8), 0: range(8), 1: range(3)}[d_lat]
        cols = {-1: range(13, 16), 0: range(16), 1: range(3)}[d_lon]
        place = first
        for i in rows:
            for j in cols:
                key_coord[0, place], key_coord[1, place] = i + d_lat * ROWS, j + d_lon * COLS
                if d_lon != 0:
                    select[place - 224, i * COLS + j] = 1.0
                place += 1
    return key_coord, select


KEY_COORD, SELECT = geometry()


def place():
    return lax.axis_index("lat"), lax.axis_index("lon")


def at(lat, lon, d_lat, d_lon):
    return (lax.rem(lat + d_lat + 8, 8), lax.rem(lon + d_lon + 32, 32))


def dot(a, b, dims=((1,), (0,))):
    return lax.dot_general(a, b, (dims, ((), ())), preferred_element_type=F32)


def norm_parts(x):
    mean = jnp.mean(x, axis=-1, keepdims=True)
    centred = x - mean
    var = jnp.mean(centred * centred, axis=-1, keepdims=True)
    return centred, lax.rsqrt(var + EPS)


def split_heads(pair):
    low = lax.broadcasted_iota(jnp.int32, pair.shape, 1) < HEAD_DIM
    zero = jnp.zeros_like(pair)
    return jnp.concatenate([jnp.where(low, pair, zero), jnp.where(low, zero, pair)], axis=0)


def join_heads(both):
    low = lax.broadcasted_iota(jnp.int32, (CELLS, 2 * HEAD_DIM), 1) < HEAD_DIM
    return jnp.where(low, both[:CELLS], both[CELLS:])


def chip():
    lat, lon = place()
    x = 2 * lax.rem(lat, 2) + lax.rem(lax.div(lon, 2), 2)
    return x, lax.div(lat, 2), lax.div(lon, 4), lax.rem(lon, 2)


def device(x, y, z, core):
    return (2 * y + lax.div(x, 2), 4 * z + 2 * lax.rem(x, 2) + core)


def turn(index, step, count):
    return lax.rem(index + step, count)


def owners():
    x, y, z, core = chip()
    x_high, x_low = lax.div(x, 2), lax.rem(x, 2)
    for d in range(1, 16):
        to_core = 1 - core if d // 8 else core
        to_high = 1 - x_high if (d // 4) % 2 else x_high
        yield device(2 * to_high + x_low, turn(y, d % 4, 4), z, to_core), to_core


def across():
    x, y, z, core = chip()
    x_high, x_low = lax.div(x, 2), lax.rem(x, 2)
    for d in range(1, 16):
        to_low = 1 - x_low if d % 2 else x_low
        yield device(2 * x_high + to_low, y, turn(z, d // 2, 8), core)


def greet():
    lat, lon = place()
    x, y, z, core = chip()
    peers = [to for to, _ in owners()] + list(across()) + [device(3 - x, y, z, core)]
    peers += [at(lat, lon, d_lat, d_lon) for _, _, d_lat, d_lon in SEGMENTS if d_lon != 0]
    barrier = pltpu.get_barrier_semaphore()
    for to in peers:
        pl.semaphore_signal(barrier, inc=1, device_id=to, device_id_type=MESH)
    return barrier, len(peers)


X_FIRST = (True, False, False, True)
EARLY, LATE = (0, 2), (1, 3)


def slot_of(core, late, index, x_low):
    part = 2 * core + late
    x, y = 2 * (index // 4) + x_low, index % 4
    return (part, x, y) if X_FIRST[part] else (part, y, x)


class Sender:
    def __init__(self, send_sem, recv_sem):
        self.send_sem, self.recv_sem, self.count = send_sem, recv_sem, 0

    def __call__(self, src, dst, to):
        copy = pltpu.make_async_remote_copy(
            src_ref=src,
            dst_ref=dst,
            send_sem=self.send_sem.at[self.count],
            recv_sem=self.recv_sem.at[self.count],
            device_id=to,
            device_id_type=MESH,
        )
        copy.start()
        self.count += 1
        return copy


class Layer:
    def __init__(self, l, b, send, loads):
        self.l, self.b, self.send, self.loads = l, b, send, loads
        self.copies, self.vec_copies, self.pending = [], [], [0, 1, 2, 3]
        self.late_copies = []
        self.shares, self.moves = [], {EARLY: [], LATE: [], "z": []}

    def load(self, n):
        if n in self.pending:
            self.pending.remove(n)
            self.loads[n].wait()

    def forward_start(self, x, before_send):
        b, l = self.b, self.l
        lat, lon = place()
        centred, rstd = norm_parts(x)
        normed = (centred * rstd * b["gain"][l : l + 1, :]).astype(BF16)
        b["normed"][l] = normed
        for n, which in enumerate((0, 3)):
            self.load(which)
            lanes = slice(INNER * n, INNER * n + INNER)
            block = dot(normed, b["win"][l, :, INNER + INNER * n : 2 * INNER + INNER * n]).astype(BF16)
            b["kv"][l, 0:CELLS, lanes] = block
            b["pack"][l, :, lanes] = dot(b["sel"][...], block).astype(BF16)
            if n == 0:
                before_send()
            lanes = pl.ds(INNER * n, INNER)
            for first, rows, d_lat, d_lon in SEGMENTS:
                if d_lon == 0:
                    source = b["kv"].at[l, pl.ds(80 if d_lat < 0 else 0, rows), lanes]
                else:
                    source = b["pack"].at[l, pl.ds(first - 224, rows), lanes]
                to = at(lat, lon, -d_lat, -d_lon)
                move = self.send(source, b["kv"].at[l, pl.ds(first, rows), lanes], to)
                (self.late_copies if n else self.copies).append(move)
        self.load(1)
        b["q"][l] = dot(normed, b["win"][l, :, :INNER]).astype(BF16)
        self.expand()

    def expand(self):
        b, l = self.b, self.l
        lat, lon = place()
        key_i = b["coord"][0:1, :]
        row_ok = (lat * ROWS + key_i >= 0) & (lat * ROWS + key_i < 64)
        step_lat = jnp.where(row_ok, key_i, 1000) - lax.broadcasted_iota(jnp.int32, (ROWS, KEYS), 0)
        step_lon = b["coord"][1:2, :] - lax.broadcasted_iota(jnp.int32, (COLS, KEYS), 0)
        bias, rw, dense = b["bias"], b["rw"], b["dense"]

        def step(head, _):
            for w in range(WIN):
                acc = jnp.full((ROWS, KEYS), -jnp.inf, F32)
                for u in range(WIN):
                    acc = jnp.where(step_lat == u - RADIUS, bias[l, head, u * WIN + w], acc)
                rw[w] = acc
            for i in range(ROWS):
                acc = jnp.full((COLS, KEYS), -jnp.inf, F32)
                for w in range(WIN):
                    acc = jnp.where(step_lon == w - RADIUS, rw[w, i : i + 1, :], acc)
                dense[head, i * COLS : (i + 1) * COLS, :] = acc
            return 0

        lax.fori_loop(0, HEADS, step, 0)

    def wait(self):
        for copy in self.copies:
            copy.wait()
        self.copies = []

    def forward_end(self, x):
        b, l = self.b, self.l
        self.wait()
        kv = b["kv"]
        for pair in range(HEADS // 2):
            lanes = slice(pair * 128, pair * 128 + 128)
            queries = split_heads(b["q"][l, :, lanes])
            bias = b["dense"][2 * pair : 2 * pair + 2].reshape(2 * CELLS, KEYS)
            scores = dot(queries, kv[l, :, lanes], ((1,), (1,))) * HEAD_DIM ** (-0.5) + bias
            top = jnp.max(scores, axis=-1, keepdims=True)
            weight = jnp.exp(scores - top)
            probs = weight / jnp.sum(weight, axis=-1, keepdims=True)
            b["probs"][l, 2 * pair : 2 * pair + 2] = probs.reshape(2, CELLS, KEYS)
        self.copies, self.late_copies = self.late_copies, []
        self.wait()
        for pair in range(HEADS // 2):
            lanes = slice(pair * 128, pair * 128 + 128)
            probs = b["probs"][l, 2 * pair : 2 * pair + 2].reshape(2 * CELLS, KEYS)
            values = kv[l, :, INNER + pair * 128 : INNER + pair * 128 + 128]
            b["mixed"][l, :, lanes] = join_heads(dot(probs.astype(BF16), values)).astype(BF16)
        self.load(2)
        return (x + dot(b["mixed"][l], b["wout"][l])).astype(BF16)

    def mixed_grad(self, up):
        self.b["gm"][self.l] = dot(up, self.b["wout"][self.l], ((1,), (1,))).astype(BF16)

    def backward_start(self):
        b, l = self.b, self.l
        lat, lon = place()
        scale = HEAD_DIM ** (-0.5)
        kv, packed, part, out = b["kv"], b["packed"], b["part"], b["out"]
        for pair in range(HEADS // 2):
            lanes = slice(pair * 128, pair * 128 + 128)
            vlanes = slice(INNER + pair * 128, INNER + pair * 128 + 128)
            keys = kv[l, :, lanes]
            grads = split_heads(b["gm"][l, :, lanes])
            grad_probs = dot(grads, kv[l, :, vlanes], ((1,), (1,)))
            probs = b["probs"][l, 2 * pair : 2 * pair + 2].reshape(2 * CELLS, KEYS)
            delta = jnp.sum(probs * grad_probs, axis=-1, keepdims=True)
            grad_scores = probs * (grad_probs - delta)
            b["dense"][2 * pair : 2 * pair + 2] = grad_scores.reshape(2, CELLS, KEYS)
            low = grad_scores.astype(BF16)
            packed[l, :, lanes] = (join_heads(dot(low, keys)) * scale).astype(BF16)
            grad_keys = dot(low, split_heads(b["q"][l, :, lanes]), ((0,), (0,))) * scale
            grad_values = dot(probs.astype(BF16), grads, ((0,), (0,)))
            half, k = pair // 2, 128 * (pair % 2)
            part[half, :, k : k + 128] = grad_keys[:CELLS]
            part[half, :, 256 + k : 384 + k] = grad_values[:CELLS]
            out[l, half, :, k : k + 128] = grad_keys[CELLS:].astype(BF16)
            out[l, half, :, 256 + k : 384 + k] = grad_values[CELLS:].astype(BF16)
            if k:
                for first, rows, d_lat, d_lon in SEGMENTS:
                    here = pl.ds(first - 128, rows)
                    to = at(lat, lon, d_lat, d_lon)
                    move = self.send(out.at[l, half, here], b["into"].at[l, half, here], to)
                    self.copies.append(move)
        self.share_packed((0,))

    def collect(self):
        b, l = self.b, self.l
        key_i = jnp.broadcast_to(b["coord"][0:1, :], (COLS, KEYS))
        step_lon = b["coord"][1:2, :] - lax.broadcasted_iota(jnp.int32, (COLS, KEYS), 0)
        ones = jnp.ones((8, KEYS), F32)
        sums, vec = b["sums"], b["vec"]
        sums[...] = jnp.zeros_like(sums)
        vec[l] = jnp.zeros((16, 128), F32)

        def step(head, _):
            for u in range(WIN):
                acc = jnp.zeros((COLS, KEYS), F32)
                for i in range(ROWS):
                    acc += jnp.where(
                        key_i == i + u - RADIUS, b["dense"][head, i * COLS : (i + 1) * COLS, :], 0.0
                    )
                for w in range(WIN):
                    o = u * WIN + w
                    sums[o : o + 1, :] = jnp.sum(
                        jnp.where(step_lon == w - RADIUS, acc, 0.0), axis=0, keepdims=True
                    )
            total = lax.dot_general(
                ones, sums[...], (((1,), (1,)), ((), ())),
                precision=lax.Precision.HIGHEST, preferred_element_type=F32,
            )
            vec[l, pl.ds(8 + head, 1), 0:56] = total[0:1]
            return 0

        lax.fori_loop(0, HEADS, step, 0)

    def backward_end(self, up, x):
        b, l = self.b, self.l
        part, into, packed = b["part"], b["into"], b["packed"]
        for half in range(2):
            for copy in self.copies[8 * half : 8 * half + 8]:
                copy.wait()
            part[half, 80:128, :] += into[l, half, 0:48, :].astype(F32)
            part[half, 0:48, :] += into[l, half, 48:96, :].astype(F32)
            total = part[half] + dot(b["sel"][...], into[l, half, 96:224, :], ((0,), (0,)))
            packed[l, :, INNER + 256 * half : INNER + 256 * half + 256] = total[:, :256].astype(BF16)
            packed[l, :, 2 * INNER + 256 * half : 2 * INNER + 256 * half + 256] = total[:, 256:].astype(BF16)
        self.copies = []
        self.share_packed((1, 2))
        grad_normed = dot(packed[l], b["win"][l], ((1,), (1,)))
        centred, rstd = norm_parts(x)
        unit = centred * rstd
        gain_grad = jnp.sum(grad_normed * unit, axis=0, keepdims=True)
        for k in range(8):
            b["vec"][l, k : k + 1, :] = gain_grad[:, k * 128 : k * 128 + 128]
        scaled = grad_normed * b["gain"][l : l + 1, :]
        mean_a = jnp.mean(scaled, axis=-1, keepdims=True)
        mean_b = jnp.mean(scaled * unit, axis=-1, keepdims=True)
        return (up.astype(F32) + rstd * (scaled - mean_a - unit * mean_b)).astype(BF16)

    def share_early(self):
        x, y, z, core = chip()
        l, b = self.l, self.b
        to, there = device(x, y, z, 1 - core), pl.ds(CELLS, CELLS)
        self.shares = [
            self.send(b["normed"].at[l], b["nb"].at[l, there], to),
            self.send(b["mixed"].at[l], b["mb"].at[l, there], to),
            self.send(self.columns(b["up"], 1 - core, 512, 0), b["ub"].at[l, there], to),
        ]
        b["nb"][l, :CELLS] = b["normed"][l]
        b["mb"][l, :CELLS] = b["mixed"][l]
        b["ub"][l, :CELLS] = self.columns(b["up"], core, 512, 0)[...]

    def columns(self, ref, core, width, start):
        return ref.at[self.l, :, pl.ds(pl.multiple_of(core * width + start, 128), width)]

    def share_packed(self, blocks):
        x, y, z, core = chip()
        l, b = self.l, self.b
        to, there = device(x, y, z, 1 - core), pl.ds(CELLS, CELLS)
        for k in blocks:
            cols = slice(256 * k, 256 * k + 256)
            source = self.columns(b["packed"], 1 - core, 256, 512 * k)
            self.shares.append(self.send(source, b["gb"].at[l, there, pl.ds(256 * k, 256)], to))
            b["gb"][l, :CELLS, cols] = self.columns(b["packed"], core, 256, 512 * k)[...]

    def product_early(self):
        l, b = self.l, self.b
        for copy in self.shares:
            copy.wait()
        self.shares = []
        slab = b["slab"]

        def step(k, _):
            for zz in range(2):
                z = 2 * k + zz
                left = b["nb"][l, :, pl.ds(pl.multiple_of(z * 128, 128), 128)]
                term = dot(left, b["gb"][l, :, 0:256], ((0,), (0,))).astype(BF16)
                for x_low in range(2):
                    for rg in range(4):
                        for cg in range(2):
                            part, f, g = slot_of(rg // 2, 0, (rg % 2) * 2 + cg, x_low)
                            row = x_low * 64 + rg * 16
                            slab[l, part, f, g, z] = term[row : row + 16, cg * 128 : cg * 128 + 128]
            left = b["mb"][l, :, pl.ds(pl.multiple_of(k * 128, 128), 128)]
            term = dot(left, b["ub"][l], ((0,), (0,))).astype(BF16)
            for zz in range(2):
                for x_low in range(2):
                    for core in range(2):
                        for cg in range(4):
                            part, f, g = slot_of(core, 0, 4 + cg, x_low)
                            row = zz * 64 + x_low * 32 + core * 16
                            slab[l, part, f, g, 2 * k + zz] = term[
                                row : row + 16, cg * 128 : cg * 128 + 128
                            ]
            return 0

        lax.fori_loop(0, 4, step, 0)
        self.start_first(EARLY)

    def product_late(self):
        l, b = self.l, self.b
        for copy in self.shares:
            copy.wait()
        self.shares = []
        slab = b["slab"]

        def step(z, _):
            left = b["nb"][l, :, pl.ds(pl.multiple_of(z * 128, 128), 128)]
            term = dot(left, b["gb"][l, :, 256:768], ((0,), (0,))).astype(BF16)
            for x_low in range(2):
                for rg in range(4):
                    for cg in range(4):
                        part, f, g = slot_of(rg // 2, 1, (rg % 2) * 4 + cg, x_low)
                        row = x_low * 64 + rg * 16
                        slab[l, part, f, g, z] = term[row : row + 16, cg * 128 : cg * 128 + 128]
            return 0

        lax.fori_loop(0, 8, step, 0)
        self.start_first(LATE)

    def start_first(self, parts):
        l, b = self.l, self.b
        x, y, z, core = chip()
        for d in (2, 1, 3):
            for t in parts:
                f = x if X_FIRST[t] else y
                to = device(turn(x, d, 4), y, z, core) if X_FIRST[t] else device(x, turn(y, d, 4), z, core)
                self.moves[parts].append(
                    self.send(b["slab"].at[l, t, turn(f, d, 4)], b["r1"].at[l, t, d - 1], to)
                )

    def arrive(self, key):
        for copy in self.moves[key]:
            copy.wait()
        self.moves[key] = []

    def first_axis(self, parts):
        self.arrive(parts)
        l, b = self.l, self.b
        slab, r1 = b["slab"], b["r1"]
        x, y, z, core = chip()
        for t in parts:
            f = x if X_FIRST[t] else y
            total = slab[l, t, f].astype(F32)
            for k in range(3):
                total += r1[l, t, k].astype(F32)
            slab[l, t, f] = total.astype(BF16)
        for d in (2, 1, 3):
            for t in parts:
                f, g = (x, y) if X_FIRST[t] else (y, x)
                to = device(x, turn(y, d, 4), z, core) if X_FIRST[t] else device(turn(x, d, 4), y, z, core)
                self.moves[parts].append(
                    self.send(slab.at[l, t, f, turn(g, d, 4)], b["r2"].at[l, t, d - 1], to)
                )

    def second_axis(self, parts):
        self.arrive(parts)
        l, b = self.l, self.b
        slab, r2 = b["slab"], b["r2"]
        x, y, z, core = chip()
        for t in parts:
            f, g = (x, y) if X_FIRST[t] else (y, x)
            total = slab[l, t, f, g].astype(F32)
            for k in range(3):
                total += r2[l, t, k].astype(F32)
            b["zs"][l, :, t] = total.astype(BF16)

    def start_third(self):
        l, b = self.l, self.b
        x, y, z, core = chip()
        b["zr"][l, z] = b["zs"][l, z]
        for d in (4, 3, 5, 2, 6, 1, 7):
            to = turn(z, d, 8)
            self.moves["z"].append(
                self.send(b["zs"].at[l, to], b["zr"].at[l, z], device(x, y, to, core))
            )

    def third_axis(self):
        self.arrive("z")
        l, b = self.l, self.b
        x, y, z, core = chip()
        total = b["zr"][l, 0].astype(F32)
        for k in range(1, 8):
            total += b["zr"][l, k].astype(F32)
        b["fin"][l] = total.astype(BF16)
        own = 8 * core + 4 * lax.div(x, 2) + y
        b["ag"][l, own] = b["fin"][l, pl.ds(2 * core, 2)]
        for to, to_core in owners():
            self.moves["z"].append(
                self.send(b["fin"].at[l, pl.ds(2 * to_core, 2)], b["ag"].at[l, own], to)
            )

    def finish(self):
        self.arrive("z")

    def small_first(self):
        l, b = self.l, self.b
        x, y, z, core = chip()
        own = 8 * core + 4 * lax.div(x, 2) + y
        b["va"][l, own] = b["vec"][l]
        for to, _ in owners():
            self.vec_copies.append(self.send(b["vec"].at[l], b["va"].at[l, own], to))

    def small_second(self):
        l, b = self.l, self.b
        x, y, z, core = chip()
        for copy in self.vec_copies:
            copy.wait()
        total = b["va"][l, 0]
        for k in range(1, 16):
            total += b["va"][l, k]
        b["vec"][l] = total
        own = 2 * z + lax.rem(x, 2)
        b["vb"][l, own] = total
        self.vec_copies = [self.send(b["vec"].at[l], b["vb"].at[l, own], to) for to in across()]

    def small_end(self):
        l, b = self.l, self.b
        for copy in self.vec_copies:
            copy.wait()
        self.vec_copies = []
        total = b["vb"][l, 0]
        for k in range(1, 16):
            total += b["vb"][l, k]
        b["small"][l] = total


TILE = (16, 128)
INPUTS = ("x_hbm", "up_hbm", "win_hbm", "wout_hbm", "gain_hbm", "bias", "sel_hbm", "coord_hbm")
OUTPUTS = ("y_out", "down_out", "ag", "small")
SCRATCH = {
    "gain": ((LAYERS, D), F32),
    "sel": ((128, CELLS), BF16),
    "coord": ((8, KEYS), jnp.int32),
    "x": ((LAYERS, CELLS, D), BF16),
    "up": ((LAYERS, CELLS, D), BF16),
    "win": ((LAYERS, D, 3 * INNER), BF16),
    "wout": ((LAYERS, INNER, D), BF16),
    "normed": ((LAYERS, CELLS, D), BF16),
    "q": ((LAYERS, CELLS, INNER), BF16),
    "kv": ((LAYERS, KEYS, D), BF16),
    "pack": ((LAYERS, 128, D), BF16),
    "probs": ((LAYERS, HEADS, CELLS, KEYS), F32),
    "mixed": ((LAYERS, CELLS, INNER), BF16),
    "rw": ((WIN, ROWS, KEYS), F32),
    "dense": ((HEADS, CELLS, KEYS), F32),
    "gm": ((LAYERS, CELLS, INNER), BF16),
    "packed": ((LAYERS, CELLS, 3 * INNER), BF16),
    "part": ((2, CELLS, 512), F32),
    "out": ((LAYERS, 2, KEYS - CELLS, 512), BF16),
    "into": ((LAYERS, 2, KEYS - CELLS, 512), BF16),
    "sums": ((56, KEYS), F32),
    "nb": ((LAYERS, 2 * CELLS, D), BF16),
    "mb": ((LAYERS, 2 * CELLS, INNER), BF16),
    "ub": ((LAYERS, 2 * CELLS, 512), BF16),
    "gb": ((LAYERS, 2 * CELLS, 768), BF16),
    "slab": ((LAYERS, 4, 4, 4, 8) + TILE, BF16),
    "r1": ((LAYERS, 4, 3, 4, 8) + TILE, BF16),
    "r2": ((LAYERS, 4, 3, 8) + TILE, BF16),
    "zs": ((LAYERS, 8, 4) + TILE, BF16),
    "zr": ((LAYERS, 8, 4) + TILE, BF16),
    "fin": ((LAYERS, 4) + TILE, BF16),
    "y": ((2, CELLS, D), BF16),
    "vec": ((LAYERS, 16, 128), F32),
    "va": ((LAYERS, 16, 16, 128), F32),
    "vb": ((LAYERS, 16, 16, 128), F32),
}
SENDS = 2 * (32 + 6 + 24 + 7 + 15 + 30)


def kernel(*refs):
    names = INPUTS + OUTPUTS + tuple(SCRATCH)
    b = dict(zip(names, refs))
    load_sem, send_sem, recv_sem = refs[len(names) :]
    barrier, greeted = greet()
    pairs = [(b["x_hbm"], b["x"].at[0])]
    key_cols, value_cols, query_cols = pl.ds(INNER, INNER), pl.ds(2 * INNER, INNER), pl.ds(0, INNER)
    for l in range(LAYERS):
        for cols in (key_cols, query_cols):
            pairs.append((b["win_hbm"].at[l, :, cols], b["win"].at[l, :, cols]))
        pairs.append((b["wout_hbm"].at[l], b["wout"].at[l]))
    pairs.append((b["up_hbm"], b["up"].at[1]))
    pairs += [(b[name + "_hbm"], b[name]) for name in ("gain", "sel", "coord")]
    pairs += [(b["win_hbm"].at[l, :, value_cols], b["win"].at[l, :, value_cols]) for l in range(LAYERS)]
    loads = [pltpu.make_async_copy(src, dst, load_sem.at[n]) for n, (src, dst) in enumerate(pairs)]
    for n in (0, 8, 1, 11, 9, 10):
        loads[n].start()
    send = Sender(send_sem, recv_sem)
    first = Layer(0, b, send, loads[1:4] + loads[11:12])
    second = Layer(1, b, send, loads[4:7] + loads[12:13])
    for n in (0, 8, 9, 10):
        loads[n].wait()
    x = b["x"][0].astype(F32)

    def begin():
        for n in (2, 3, 4, 12, 5, 7, 6):
            loads[n].start()
        pl.semaphore_wait(barrier, greeted)

    first.forward_start(x, begin)
    b["x"][1] = first.forward_end(x)
    x = b["x"][1].astype(F32)
    second.forward_start(x, lambda: None)
    loads[7].wait()
    second.load(2)
    second.mixed_grad(b["up"][1])
    b["y"][0] = second.forward_end(x)
    saves = [pltpu.make_async_copy(b["y"].at[0], b["y_out"], load_sem.at[13])]
    saves[0].start()
    second.share_early()
    second.backward_start()
    second.product_early()
    second.collect()
    b["up"][0] = second.backward_end(b["up"][1], b["x"][1].astype(F32))
    up = b["up"][0]
    first.mixed_grad(up)
    first.share_early()
    second.small_first()
    second.first_axis(EARLY)
    first.backward_start()
    second.product_late()
    first.product_early()
    first.collect()
    second.first_axis(LATE)
    second.small_second()
    b["y"][1] = first.backward_end(up, b["x"][0].astype(F32))
    saves.append(pltpu.make_async_copy(b["y"].at[1], b["down_out"], load_sem.at[14]))
    saves[1].start()
    first.product_late()
    first.small_first()
    second.second_axis(EARLY)
    second.second_axis(LATE)
    second.start_third()
    first.first_axis(EARLY)
    second.third_axis()
    second.small_end()
    first.first_axis(LATE)
    first.small_second()
    first.second_axis(EARLY)
    second.finish()
    first.second_axis(LATE)
    first.start_third()
    first.small_end()
    first.third_axis()
    first.finish()
    for save in saves:
        save.wait()


def lay_out(y_ref, down_ref, ag, small, y_out, down_out, in_out, out_out, gain_out, bias_out):
    y_out[...] = y_ref[...]
    down_out[...] = down_ref[...]
    for l in range(LAYERS):
        for slot in range(16):
            core_of, index = slot // 8, slot % 8
            early, late = ag[l, slot, 0].astype(F32), ag[l, slot, 1].astype(F32)
            if index < 4:
                row, col = 16 * (index // 2), 256 * core_of + 128 * (index % 2)
                in_out[l, row : row + 16, col : col + 128] = early
            else:
                col = core_of * 512 + (index - 4) * 128
                out_out[l, :, col : col + 128] = early
            row = 16 * (index // 4)
            col = 512 * (1 + (index % 4) // 2) + 256 * core_of + 128 * (index % 2)
            in_out[l, row : row + 16, col : col + 128] = late
        for k in range(8):
            gain_out[l : l + 1, k * 128 : k * 128 + 128] = small[l, k : k + 1, :]
        bias_out[l] = small[l, 8:16, : WIN * WIN]


def solution_step(inputs, input_weight, output_weight, norm_gain, position_bias, cotangent):
    whole, far = pl.BlockSpec(memory_space=pltpu.VMEM), pl.BlockSpec(memory_space=pl.ANY)
    scalars = pl.BlockSpec(memory_space=pltpu.SMEM)
    shape = jax.ShapeDtypeStruct
    results = pl.pallas_call(
        kernel,
        out_shape=(
            shape((CELLS, D), BF16),
            shape((CELLS, D), BF16),
            shape((LAYERS, 16, 2) + TILE, BF16),
            shape((LAYERS, 16, 128), F32),
        ),
        in_specs=[far] * 5 + [scalars, far, far],
        out_specs=(far, far, whole, whole),
        scratch_shapes=[pltpu.VMEM(*spec) for spec in SCRATCH.values()]
        + [
            pltpu.SemaphoreType.DMA((15,)),
            pltpu.SemaphoreType.DMA((SENDS,)),
            pltpu.SemaphoreType.DMA((SENDS,)),
        ],
        compiler_params=pltpu.CompilerParams(
            collective_id=0, has_side_effects=True, vmem_limit_bytes=60 * 1024 * 1024
        ),
    )(
        inputs.reshape(CELLS, D),
        cotangent.reshape(CELLS, D),
        input_weight,
        output_weight,
        norm_gain,
        position_bias,
        jnp.asarray(SELECT, BF16),
        jnp.asarray(KEY_COORD),
    )
    y, down, in_grad, out_grad, gain_grad, bias_grad = pl.pallas_call(
        lay_out,
        out_shape=(
            shape((CELLS, D), BF16),
            shape((CELLS, D), BF16),
            shape((LAYERS, 32, 1536), F32),
            shape((LAYERS, 16, 1024), F32),
            shape((LAYERS, D), F32),
            shape((LAYERS, HEADS, WIN * WIN), F32),
        ),
        in_specs=[whole] * 4,
        out_specs=(whole,) * 6,
    )(*results)
    tile = (ROWS, COLS, D)
    return y.reshape(tile), down.reshape(tile), in_grad, out_grad, gain_grad, bias_grad


def solution(mesh):
    return jax.shard_map(
        solution_step,
        mesh=mesh,
        in_specs=(P("lat", "lon", None), P(), P(), P(), P(), P("lat", "lon", None)),
        out_specs=(
            P("lat", "lon", None),
            P("lat", "lon", None),
            P(None, "lon", None),
            P(None, "lon", None),
            P(),
            P(),
        ),
        check_vma=False,
    )
```
